128 devices in a mesh: rep: 16 (over y, z), tm: 8 (over x, core).
Axes of the slice: x: 4, y: 4, z: 4, core: 2. Of those that a mesh axis runs over, the one named last changes fastest.
Arguments:
- video: bfloat16 [16, 32, 16, 32, 128], P('rep', 'tm'), may hold values from -6 to 6
- frame_counts: int32 [16], P('rep'), may hold values from 1 to 32, as said below
- first_weight: bfloat16 [3, 3, 3, 256, 256], replicated, may hold values from -0.078125 to 0.078125
- second_weight: bfloat16 [3, 512, 512], replicated, may hold values from -0.15625 to 0.15625
- cotangent: bfloat16 [16, 8, 16, 32, 512], P('rep', None, 'tm'), may hold values from -6 to 6
Outputs:
- features_out: bfloat16 [16, 8, 16, 32, 512], P('rep', None, 'tm')
- grad_input: bfloat16 [16, 32, 16, 32, 128], P('rep', 'tm')
- grad_first: float32 [6912, 256], P('rep')
- grad_second: float32 [1536, 512], P('rep')
The draws below stay inside these ranges and needn't reach their ends.
Inputs may be any that keep to these rules, and one draw needn't show every extreme that they name: `frame_counts`: at least one clip has exactly 32 live frames.
All inputs are finite; a program needn't handle non-finite values.
Results may differ from the reference program's by a relative error of at most 0.013.
Values may be sent and summed in bfloat16 or wider, within the bound.
A program may use at most 128 MiB of HBM per device.

```python
import math
import jax
import jax.numpy as jnp
from jax import lax

C0 = 128
C1 = 256
C2 = 512
W = 32
CLIPS = 16
FRAMES = 32
H = 16


def draw_frame_counts(key, part):
    key = jax.random.fold_in(key, 11)
    first_key, second_key = jax.random.split(key)
    counts = jax.random.randint(first_key, (CLIPS,), 1, FRAMES + 1)
    longest = jax.random.randint(second_key, (), 0, CLIPS)
    return jnp.where(jnp.arange(CLIPS) == longest, FRAMES, counts).astype(jnp.int32)


def levels(stream_key, dims, cuts, smallest, top_value):
    def one(position, parts):
        steps = jax.random.uniform(jax.random.fold_in(jax.random.fold_in(stream_key, 6), position), (parts,), jnp.float32, smallest / len(cuts), top_value / len(cuts))
        return jnp.repeat(jnp.exp(steps), dims[position] // parts).reshape((-1,) + (1,) * (len(dims) - position - 1))

    gain = one(*cuts[0])
    for cut in cuts[1:]:
        gain = gain * one(*cut)
    return gain


def bell_draw(key, extent, scale, bound, shards=(), held_as=jnp.bfloat16):
    drawn = jax.random.normal(key, extent, jnp.float32) * scale
    if len(shards) > 0:
        drawn = levels(key, extent, shards, -0.22, 0.18) * drawn
    return jnp.clip(drawn, min=-bound, max=bound).astype(held_as)


def setup_inputs(seed: int = 0) -> dict:
    key_of = jax.random.split(jax.random.key(seed), 6)
    video = bell_draw(key_of[0], (CLIPS, FRAMES, H, W, C0), 1.0, 6.0, ((0, 16), (1, 8)))
    frame_counts = draw_frame_counts(jax.random.fold_in(key_of[5], 71), 0)
    first_weight = bell_draw(key_of[2], (3, 3, 3, C1, C1), (27 * C1) ** -0.5, 0.078125)
    second_weight = bell_draw(key_of[3], (3, C2, C2), (3 * C2) ** -0.5, 0.15625)
    cotangent = bell_draw(key_of[4], (CLIPS, FRAMES // 4, H, W, C2), 1.0, 6.0, ((0, 16), (2, 8)))
    return dict(video=video, frame_counts=frame_counts, first_weight=first_weight, second_weight=second_weight, cotangent=cotangent)


root_half = 0.7071067811865476

def haar_pairs(frames_block):
    paired = frames_block.astype(jnp.float32).reshape((frames_block.shape[0] // 2, 2) + frames_block.shape[1:])
    first_frame = paired[:, 0]
    second_frame = paired[:, 1]
    return jnp.concatenate([(first_frame + second_frame) * root_half, (first_frame - second_frame) * root_half], axis=-1).astype(jnp.bfloat16)

def haar_back(gradient):
    half_width = gradient.shape[-1] // 2
    low_band = gradient[..., :half_width]
    high_band = gradient[..., half_width:]
    joined = jnp.stack([(low_band + high_band) * root_half, (low_band - high_band) * root_half], axis=1)
    return joined.reshape((gradient.shape[0] * 2,) + gradient.shape[1:-1] + (half_width,))

def silu_slope(activation):
    sigmoid_val = jax.nn.sigmoid(activation)
    return sigmoid_val * (1.0 + activation * (1.0 - sigmoid_val))

def reference(video, frame_counts, first_weight, second_weight, cotangent):
    half_frames = FRAMES // 2
    quarter = FRAMES // 4

    def one_clip(totals, inputs):
        clip_frames, frame_count, grad_out = inputs
        keep_mask = (jnp.arange(FRAMES, dtype=jnp.int32) < frame_count)[:, None, None, None]
        masked = jnp.where(keep_mask, clip_frames, jnp.zeros_like(clip_frames))
        first_haar = haar_pairs(masked)
        padded = jnp.pad(first_haar, ((2, 0), (1, 1), (1, 1), (0, 0)))
        pre_act = jnp.zeros((half_frames * H * W, C1), jnp.float32)
        for tap_t in range(3):
            for tap_y in range(3):
                for tap_x in range(3):
                    window_rows = padded[tap_t:tap_t + half_frames, tap_y:tap_y + H, tap_x:tap_x + W].reshape(-1, C1)
                    pre_act = pre_act + jnp.dot(window_rows, first_weight[tap_t, tap_y, tap_x], preferred_element_type=jnp.float32)
        hidden = jax.nn.silu(pre_act).astype(jnp.bfloat16).reshape(half_frames, H, W, C1)
        second_haar = haar_pairs(hidden)
        shifted = jnp.pad(second_haar, ((2, 0), (0, 0), (0, 0), (0, 0)))
        grad_flat_out = grad_out.reshape(-1, C2)
        features = jnp.zeros((quarter * H * W, C2), jnp.float32)
        second_parts = []
        for tap_t in range(3):
            window_rows = shifted[tap_t:tap_t + quarter].reshape(-1, C2)
            features = features + jnp.dot(window_rows, second_weight[tap_t], preferred_element_type=jnp.float32)
            second_parts.append(jnp.dot(window_rows.T, grad_flat_out, preferred_element_type=jnp.float32))
        later_pad = jnp.pad(grad_out, ((0, 2), (0, 0), (0, 0), (0, 0)))
        grad_haar2 = jnp.zeros((quarter * H * W, C2), jnp.float32)
        for tap_t in range(3):
            window_rows = later_pad[2 - tap_t:2 - tap_t + quarter].reshape(-1, C2)
            grad_haar2 = grad_haar2 + jnp.dot(window_rows, second_weight[tap_t].T, preferred_element_type=jnp.float32)
        grad_hidden = haar_back(grad_haar2.reshape(quarter, H, W, C2)).astype(jnp.bfloat16)
        grad_pre = (grad_hidden.astype(jnp.float32) * silu_slope(pre_act.reshape(half_frames, H, W, C1))).astype(jnp.bfloat16)
        grad_flat = grad_pre.reshape(-1, C1)
        grad_padded = jnp.pad(grad_pre, ((0, 2), (1, 1), (1, 1), (0, 0)))
        grad_haar1 = jnp.zeros((half_frames * H * W, C1), jnp.float32)
        first_parts = []
        for tap_t in range(3):
            for tap_y in range(3):
                for tap_x in range(3):
                    window_rows = padded[tap_t:tap_t + half_frames, tap_y:tap_y + H, tap_x:tap_x + W].reshape(-1, C1)
                    first_parts.append(jnp.dot(window_rows.T, grad_flat, preferred_element_type=jnp.float32))
                    back_rows = grad_padded[2 - tap_t:2 - tap_t + half_frames, 2 - tap_y:2 - tap_y + H, 2 - tap_x:2 - tap_x + W].reshape(-1, C1)
                    grad_haar1 = grad_haar1 + jnp.dot(back_rows, first_weight[tap_t, tap_y, tap_x].T, preferred_element_type=jnp.float32)
        grad_input = jnp.where(keep_mask, haar_back(grad_haar1.reshape(half_frames, H, W, C1)), 0.0).astype(jnp.bfloat16)
        totals = (totals[0] + jnp.concatenate(first_parts, axis=0), totals[1] + jnp.concatenate(second_parts, axis=0))
        return (totals, (features.astype(jnp.bfloat16).reshape(quarter, H, W, C2), grad_input))
    initial = (jnp.zeros((27 * C1, C1), jnp.float32), jnp.zeros((3 * C2, C2), jnp.float32))
    totals, outputs = lax.scan(one_clip, initial, (video, frame_counts, cotangent))
    scale_first = 1.0 / math.sqrt(CLIPS * (FRAMES // 2) * H * W)
    scale_second = 1.0 / math.sqrt(CLIPS * (FRAMES // 4) * H * W)
    return (outputs[0], outputs[1], totals[0] * scale_first, totals[1] * scale_second)
```

```python
import functools
import math

import jax
import jax.numpy as jnp
from jax import lax
from jax.experimental import pallas as pl
from jax.experimental.pallas import tpu as pltpu
from jax.sharding import PartitionSpec as P

root_half = 0.7071067811865476
MESH = pl.DeviceIdType.MESH
bf16 = jnp.bfloat16
f32 = jnp.float32

NY, NZ, NX = 4, 4, 4
ROWS_F, ROWS_S = 432, 192
ROWS = ROWS_F + ROWS_S
PIECE = 160


def dot(a, b):
    return jnp.dot(a, b, preferred_element_type=f32)


def dot_nt(a, b):
    return lax.dot_general(a, b, (((1,), (1,)), ((), ())), preferred_element_type=f32)


def put_shifted(dst, index, read, flip):
    lanes = (512, 0) if flip else (0, 512)
    zero_row = jnp.zeros((32, 768), bf16)
    dst[index, 0] = zero_row
    dst[index, 17] = zero_row

    def chunk(n, carry):
        value = read(pl.ds(pl.multiple_of(n * 64, 64), 64))
        rows = value.astype(f32).reshape(2, 32, 256)
        column = lax.broadcasted_iota(jnp.int32, (2, 32, 256), 1)
        before = jnp.where(column == 0, 0.0, pltpu.roll(rows, 1, 1)).astype(bf16)
        after = jnp.where(column == 31, 0.0, pltpu.roll(rows, 31, 1)).astype(bf16)
        at = pl.ds(1 + 2 * n, 2)
        dst[index, at, :, lanes[0] : lanes[0] + 256] = before
        dst[index, at, :, 256:512] = value.reshape(2, 32, 256)
        dst[index, at, :, lanes[1] : lanes[1] + 256] = after
        return carry

    lax.fori_loop(0, 8, chunk, 0)


def kernel(
    video, counts, first_w, second_w, cotangent,
    feat_out, input_out, first_out, second_out,
    vid, w1, w1t, w2, ctp, cts, ct_t, hown, hin, hex_, xs, acc, ghs, ghr, hs, hr, sh,
    gpo, gps, gph, gp_t, gpx, pf, ps, r1, s1, r2, s2, r3, s3, ag, fout, gout, gfo, gso,
    load_sem, halo_s, halo_r, cts_s, cts_r, ex_s, ex_r, gh_s, gh_r, h_s, h_r, sh_s, sh_r,
    gp_s, gp_r, gph_s, gph_r, f1_s, f1_r, c1_s, c1_r, p2_s, p2_r, p3_s, p3_r, p4_s, p4_r, out_sem,
):
    rep = lax.axis_index("rep")
    tm = lax.axis_index("tm")
    y, z = rep // NZ, rep % NZ
    x, c = tm // 2, tm % 2

    def remote(src, dst, send, recv, to):
        return pltpu.make_async_remote_copy(
            src_ref=src, dst_ref=dst, send_sem=send, recv_sem=recv, device_id=to, device_id_type=MESH
        )

    def device(to_x, to_y, to_z, to_c):
        return (to_y * NZ + to_z, to_x * 2 + to_c)

    sibling = (rep, x * 2 + 1 - c)

    loads = [
        pltpu.make_async_copy(video, vid, load_sem.at[0]),
        pltpu.make_async_copy(cotangent, ctp.at[pl.ds(0, 8)], load_sem.at[1]),
        pltpu.make_async_copy(second_w, w2, load_sem.at[2]),
        pltpu.make_async_copy(first_w, w1, load_sem.at[3]),
    ]
    for load in loads:
        load.start()

    barrier = pltpu.get_barrier_semaphore()
    partners = [(rep, (tm + k) % 8) for k in range(1, 8)]
    for k in range(1, 4):
        for core in range(2):
            partners.append(device(x, (y + k) % NY, z, core))
            partners.append(device(x, y, (z + k) % NZ, core))
    for partner in partners:
        pl.semaphore_signal(barrier, inc=1, device_id=partner, device_id_type=MESH)

    live = counts[0]
    loads[0].wait()

    def keep(frame):
        return jnp.where(tm * 4 + frame < live, 1.0, 0.0).astype(f32)

    for t in range(2):
        even, odd = keep(2 * t), keep(2 * t + 1)

        def pair(n, carry):
            at = pl.ds(pl.multiple_of(n * 64, 64), 64)
            one = vid[2 * t, at].astype(f32) * even
            two = vid[2 * t + 1, at].astype(f32) * odd
            hown[t, at, 0:128] = ((one + two) * root_half).astype(bf16)
            hown[t, at, 128:256] = ((one - two) * root_half).astype(bf16)
            return carry

        lax.fori_loop(0, 8, pair, 0)

    pl.semaphore_wait(barrier, len(partners))

    following = (rep, (tm + 1) % 8)
    halo = [
        remote(hown.at[t], hin.at[t], halo_s.at[t], halo_r.at[t], following) for t in range(2)
    ]
    halo[1].start()
    halo[0].start()
    loads[1].wait()
    give_ct = remote(ctp.at[pl.ds(0, 8)], cts, cts_s, cts_r, sibling)
    give_ct.start()

    ctp[8:10] = jnp.zeros((2, 64, 512), bf16)
    loads[2].wait()

    def back_step(n, carry):
        grad = jnp.zeros((128, 512), f32)
        for a in range(3):
            grad = grad + dot_nt(ctp[pl.ds(2 * n + 2 - a, 2)].reshape(128, 512), w2[a])
        low, high = grad[:, :256], grad[:, 256:]
        ghs[pl.ds(2 * n, 2), 0] = ((low + high) * root_half).astype(bf16).reshape(2, 64, 256)
        ghs[pl.ds(2 * n, 2), 1] = ((low - high) * root_half).astype(bf16).reshape(2, 64, 256)
        return carry

    lax.fori_loop(0, 4, back_step, 0)

    def exchange(source, slots, send, recv):
        copies = []
        for k in range(1, 8):
            to = (tm + k) % 8
            copies.append(remote(source.at[to], slots.at[tm], send.at[to], recv.at[tm], (rep, to)))
            copies[-1].start()
        slots[tm] = source[tm]
        return copies

    def arrived(slots, recv):
        for k in range(1, 8):
            peer = (tm + k) % 8
            remote(slots.at[peer], slots.at[peer], recv.at[peer], recv.at[peer], (rep, peer)).wait_recv()

    gh_copies = exchange(ghs, ghr, gh_s, gh_r)

    base = 2 * c
    for t in range(2):
        put_shifted(xs, base + 2 + t, lambda at, t=t: hown[t, at], False)
    loads[3].wait()

    def window(frame, b):
        return xs[base + frame, pl.ds(b, 16)].reshape(512, 768)

    acc[...] = jnp.zeros_like(acc)

    def own_taps(b, carry):
        acc[0] += dot(window(2, b), w1[6 + b])
        acc[1] += dot(window(2, b), w1[3 + b]) + dot(window(3, b), w1[6 + b])
        return carry

    lax.fori_loop(0, 3, own_taps, 0)

    def turn_tap(n, carry):
        for d in range(3):
            w1t[n, 256 * d : 256 * d + 256] = w1[n, 256 * d : 256 * d + 256].T
        return carry

    lax.fori_loop(0, 9, turn_tap, 0)
    ct_t[:, 0:512] = ctp[0:8].reshape(512, 512).T

    for copy in halo:
        copy.wait_recv()
    to_sibling = remote(hin.at[1], hex_, ex_s, ex_r, sibling)

    @pl.when(c == 0)
    def _():
        remote(hin.at[1], hex_, ex_s, ex_r, sibling).start()

    @pl.when(c == 1)
    def _():
        remote(hown.at[0], hex_, ex_s, ex_r, sibling).start()

    inside = jnp.where(tm > 0, 1.0, 0.0).astype(bf16)
    for t in range(2):
        put_shifted(xs, base + t, lambda at, t=t: hin[t, at] * inside, False)

    def halo_taps(b, carry):
        acc[0] += dot(window(0, b), w1[b]) + dot(window(1, b), w1[3 + b])
        acc[1] += dot(window(1, b), w1[b])
        return carry

    lax.fori_loop(0, 3, halo_taps, 0)

    def activate(n, carry):
        at = pl.ds(pl.multiple_of(n * 64, 64), 64)
        for t in range(2):
            value = acc[t, at]
            hs[n, t] = (value * jax.nn.sigmoid(value)).astype(bf16)
        return carry

    lax.fori_loop(0, 8, activate, 0)
    h_copies = exchange(hs, hr, h_s, h_r)

    arrived(ghr, gh_r)

    def slope(n, carry):
        at = pl.ds(pl.multiple_of(n * 64, 64), 64)
        for t in range(2):
            value = acc[t, at]
            gate = jax.nn.sigmoid(value)
            grad = ghr[n, t].astype(f32) * (gate * (1.0 + value * (1.0 - gate)))
            gpo[t, at] = grad.astype(bf16)
        return carry

    lax.fori_loop(0, 8, slope, 0)
    give_gp = remote(gpo, gps, gp_s, gp_r, sibling)
    give_gp.start()
    before = (rep, (tm + 7) % 8)
    give_gph = remote(gpo, gph, gph_s, gph_r, before)

    @pl.when(c == 0)
    def _():
        give_gph.start()

    to_sibling.wait_recv()
    extra_inside = jnp.where((c == 0) | (x > 0), 1.0, 0.0).astype(bf16)
    put_shifted(xs, 4 - 3 * c, lambda at: hex_[at] * extra_inside, False)
    for t in range(2):
        gp_t[:, pl.ds(pl.multiple_of((2 * c + t) * 512, 512), 512)] = gpo[t].T
    give_gp.wait_recv()
    for t in range(2):
        gp_t[:, pl.ds(pl.multiple_of((2 - 2 * c + t) * 512, 512), 512)] = gps[t].T

    def deliver(source, rows, send, recv, shard):
        to_y, to_z = 2 * c + shard // 4, shard % 4
        stops = (
            (0, r1.at[y, to_z, rows], device(x, to_y, z, 0), recv.at[y, to_z], (to_y == y) & (c == 0)),
            (1, r1.at[z, to_y, rows], device(x, y, to_z, 1), recv.at[z, to_y], (to_z == z) & (c == 1)),
        )
        for half, slot, to, sem, here in stops:

            @pl.when(here)
            def _(half=half, slot=slot, sem=sem):
                pltpu.make_async_copy(source(half, shard), slot, sem).start()

            @pl.when(jnp.logical_not(here))
            def _(half=half, slot=slot, sem=sem, to=to):
                remote(source(half, shard), slot, send.at[half, shard], sem, to).start()

    def delivered(source, rows, send, shard):
        to_y, to_z = 2 * c + shard // 4, shard % 4
        stops = ((0, (to_y == y) & (c == 0)), (1, (to_z == z) & (c == 1)))
        for half, here in stops:

            @pl.when(jnp.logical_not(here))
            def _(half=half):
                remote(
                    source(half, shard), r1.at[0, 0, rows], send.at[half, shard], send.at[half, shard], sibling
                ).wait_send()

    rows_f, rows_s = pl.ds(0, ROWS_F), pl.ds(ROWS_F, ROWS_S)

    def source_f(half, shard):
        return pf.at[half, pl.ds(pl.multiple_of(128 + ROWS_F * shard, 16), ROWS_F)]

    def source_s(half, shard):
        return ps.at[half, shard]

    def tap(j, carry):
        k = 13 * c + j
        a, b, d = k // 9, (k // 3) % 3, k % 3
        patch = xs[pl.ds(a, 4), pl.ds(b, 16), :, pl.ds(pl.multiple_of(d * 256, 256), 256)]
        turned = dot(gp_t[...], patch.reshape(2048, 256)).T.astype(bf16)
        at = pl.ds(pl.multiple_of(256 * j + 128 - 128 * c, 128), 256)
        pf[0, at] = turned[:, :128]
        pf[1, at] = turned[:, 128:]
        done = (256 * j + 128) // ROWS_F
        was = (256 * jnp.maximum(j, 1) - 128) // ROWS_F

        @pl.when(done > was)
        def _():
            deliver(source_f, rows_f, f1_s, f1_r, was)

        return carry

    lax.fori_loop(0, 14, tap, 0)

    arrived(hr, h_r)
    sh[0, 0:2] = jnp.zeros((2, 64, 512), bf16)
    sh[1, 0:2] = jnp.zeros((2, 64, 512), bf16)

    def second(n, carry):
        one, two = hr[n, 0].astype(f32), hr[n, 1].astype(f32)
        sh[0, 2 + n, :, 0:256] = ((one + two) * root_half).astype(bf16)
        sh[0, 2 + n, :, 256:512] = ((one - two) * root_half).astype(bf16)
        return carry

    lax.fori_loop(0, 8, second, 0)
    give_sh = remote(sh.at[0, pl.ds(2, 8)], sh.at[1, pl.ds(2, 8)], sh_s, sh_r, sibling)
    give_sh.start()

    def forward(n, carry):
        value = jnp.zeros((128, 512), f32)
        for a in range(3):
            value = value + dot(sh[0, pl.ds(2 * n + a, 2)].reshape(128, 512), w2[a])
        fout[pl.ds(2 * n, 2)] = value.astype(bf16).reshape(2, 64, 512)
        return carry

    lax.fori_loop(0, 4, forward, 0)
    write_feat = pltpu.make_async_copy(fout, feat_out, out_sem.at[0])
    write_feat.start()

    give_ct.wait_recv()
    ct_t[:, 512:1024] = cts[...].reshape(512, 512).T
    give_sh.wait_recv()
    for n in range(3):
        m = 3 * c + n
        a, band = m // 2, m % 2
        lanes = pl.ds(pl.multiple_of(band * 256, 256), 256)
        own = sh[0, pl.ds(a, 8), :, lanes].reshape(512, 256)
        other = sh[1, pl.ds(a, 8), :, lanes].reshape(512, 256)
        turned = (dot(ct_t[:, 0:512], own) + dot(ct_t[:, 512:1024], other)).T.astype(bf16)
        for block in range(16):
            row = 256 * n + 16 * block
            shard, at = row // 96, row % 96
            for quarter in range(4):
                ps[quarter // 2, shard, (quarter % 2) * 96 + at : (quarter % 2) * 96 + at + 16] = turned[
                    16 * block : 16 * block + 16, quarter * 128 : quarter * 128 + 128
                ]

    def send_second(shard, carry):
        deliver(source_s, rows_s, c1_s, c1_r, shard)
        return carry

    lax.fori_loop(0, 8, send_second, 0)

    for t in range(2):
        put_shifted(gpx, t, lambda at, t=t: gpo[t, at], True)

    @pl.when(c == 1)
    def _():
        give_gph.wait_recv()
        inner = jnp.where(tm < 7, 1.0, 0.0).astype(bf16)
        for t in range(2):
            put_shifted(gpx, 2 + t, lambda at, t=t: gph[t, at] * inner, True)

    @pl.when(c == 0)
    def _():
        for t in range(2):
            put_shifted(gpx, 2 + t, lambda at, t=t: gps[t, at], True)

    acc[...] = jnp.zeros_like(acc)

    def input_taps(n, carry):
        a, b = n // 3, n % 3
        for t in range(2):
            acc[t] += dot(gpx[2 - a + t, pl.ds(2 - b, 16)].reshape(512, 768), w1t[n])
        return carry

    lax.fori_loop(0, 9, input_taps, 0)
    for t in range(2):
        even, odd = keep(2 * t), keep(2 * t + 1)

        def unpair(n, carry):
            at = pl.ds(pl.multiple_of(n * 64, 64), 64)
            low, high = acc[t, at, 0:128], acc[t, at, 128:256]
            gout[2 * t, at] = ((low + high) * root_half * even).astype(bf16)
            gout[2 * t + 1, at] = ((low - high) * root_half * odd).astype(bf16)
            return carry

        lax.fori_loop(0, 8, unpair, 0)
    write_input = pltpu.make_async_copy(gout, input_out, out_sem.at[1])
    write_input.start()

    at_home = jnp.where(c == 0, z, y)

    def stop_two(k):
        to = device(x, jnp.where(c == 0, y, k), jnp.where(c == 0, k, z), c)
        return remote(s1.at[k], r2.at[at_home], p2_s.at[k], p2_r.at[at_home], to)

    def first_sum(k, carry):
        for rows, recv in ((rows_f, f1_r), (rows_s, c1_r)):
            for source in range(4):
                slot = r1.at[source, k, rows]
                pltpu.make_async_copy(slot, slot, recv.at[source, k]).wait()
            total = r1[0, k, rows].astype(f32)
            for source in range(1, 4):
                total = total + r1[source, k, rows].astype(f32)
            s1[k, rows] = total.astype(bf16)

        @pl.when(k != at_home)
        def _():
            stop_two(k).start()

        return carry

    lax.fori_loop(0, 4, first_sum, 0)
    r2[at_home] = s1[at_home]

    for k in range(1, 4):
        peer = (at_home + k) % 4
        remote(r2.at[peer], r2.at[peer], p2_r.at[peer], p2_r.at[peer], sibling).wait_recv()

    def second_sum(n, carry):
        at = pl.ds(pl.multiple_of(n * 208, 16), 208)
        total = r2[0, at].astype(f32)
        for source in range(1, 4):
            total = total + r2[source, at].astype(f32)
        s2[at] = total.astype(bf16)
        return carry

    lax.fori_loop(0, 3, second_sum, 0)
    s2[ROWS : 4 * PIECE] = jnp.zeros((4 * PIECE - ROWS, 128), bf16)

    def piece(index):
        return pl.ds(pl.multiple_of(index * PIECE, 16), PIECE)

    third = []
    for k in range(1, 4):
        to = (x + k) % 4
        third.append(remote(s2.at[piece(to)], r3.at[x], p3_s.at[k], p3_r.at[x], (rep, to * 2 + c)))
        third[-1].start()
    r3[x] = s2[piece(x)]
    for k in range(1, 4):
        peer = (x + k) % 4
        remote(r3.at[peer], r3.at[peer], p3_r.at[peer], p3_r.at[peer], sibling).wait_recv()
    total = r3[0].astype(f32)
    for source in range(1, 4):
        total = total + r3[source].astype(f32)
    s3[...] = total.astype(bf16)

    fourth = []
    for k in range(1, 8):
        to = (tm + k) % 8
        fourth.append(remote(s3, ag.at[c, piece(x)], p4_s.at[k], p4_r.at[tm], (rep, to)))
        fourth[-1].start()
    ag[c, piece(x)] = s3[...]
    for k in range(1, 8):
        peer = (tm + k) % 8
        slot = ag.at[peer % 2, piece(peer // 2)]
        remote(slot, slot, p4_r.at[peer], p4_r.at[peer], sibling).wait_recv()
    scale_first = 1.0 / math.sqrt(131072)
    scale_second = 1.0 / math.sqrt(65536)
    for half in range(2):
        gfo[:, 128 * half : 128 * half + 128] = ag[half, 0:432].astype(f32) * scale_first
        for w in range(2):
            lane = 256 * half + 128 * w
            gso[:, lane : lane + 128] = ag[half, 432 + 96 * w : 528 + 96 * w].astype(f32) * scale_second
    write_first = pltpu.make_async_copy(gfo, first_out, out_sem.at[2])
    write_second = pltpu.make_async_copy(gso, second_out, out_sem.at[3])
    write_first.start()
    write_second.start()

    for copy in halo + gh_copies + h_copies + third + fourth + [give_ct, to_sibling, give_gp, give_sh]:
        copy.wait_send()

    @pl.when(c == 0)
    def _():
        give_gph.wait_send()

    def drain(shard, carry):
        delivered(source_f, rows_f, f1_s, shard)
        delivered(source_s, rows_s, c1_s, shard)
        return carry

    lax.fori_loop(0, 8, drain, 0)

    def drain_two(k, carry):
        @pl.when(k != at_home)
        def _():
            stop_two(k).wait_send()

        return carry

    lax.fori_loop(0, 4, drain_two, 0)
    for write in (write_feat, write_input, write_first, write_second):
        write.wait()


def body(video, frame_counts, first_weight, second_weight, cotangent):
    any_ = pl.BlockSpec(memory_space=pl.ANY)
    vmem = pltpu.VMEM
    dma = pltpu.SemaphoreType.DMA
    out = pl.pallas_call(
        kernel,
        out_shape=(
            jax.ShapeDtypeStruct((8, 64, 512), bf16),
            jax.ShapeDtypeStruct((4, 512, 128), bf16),
            jax.ShapeDtypeStruct((432, 256), f32),
            jax.ShapeDtypeStruct((96, 512), f32),
        ),
        in_specs=[any_, pl.BlockSpec(memory_space=pltpu.SMEM), any_, any_, any_],
        out_specs=(any_,) * 4,
        scratch_shapes=[
            vmem((4, 512, 128), bf16),
            vmem((9, 768, 256), bf16),
            vmem((9, 768, 256), bf16),
            vmem((3, 512, 512), bf16),
            vmem((10, 64, 512), bf16),
            vmem((8, 64, 512), bf16),
            vmem((512, 1024), bf16),
            vmem((2, 512, 256), bf16),
            vmem((2, 512, 256), bf16),
            vmem((512, 256), bf16),
            vmem((6, 18, 32, 768), bf16),
            vmem((2, 512, 256), f32),
            vmem((8, 2, 64, 256), bf16),
            vmem((8, 2, 64, 256), bf16),
            vmem((8, 2, 64, 256), bf16),
            vmem((8, 2, 64, 256), bf16),
            vmem((2, 10, 64, 512), bf16),
            vmem((2, 512, 256), bf16),
            vmem((2, 512, 256), bf16),
            vmem((2, 512, 256), bf16),
            vmem((256, 2048), bf16),
            vmem((4, 18, 32, 768), bf16),
            vmem((2, 3712, 128), bf16),
            vmem((2, 8, ROWS_S, 128), bf16),
            vmem((4, 4, ROWS, 128), bf16),
            vmem((4, ROWS, 128), bf16),
            vmem((4, ROWS, 128), bf16),
            vmem((4 * PIECE, 128), bf16),
            vmem((4, PIECE, 128), bf16),
            vmem((PIECE, 128), bf16),
            vmem((2, 4 * PIECE, 128), bf16),
            vmem((8, 64, 512), bf16),
            vmem((4, 512, 128), bf16),
            vmem((432, 256), f32),
            vmem((96, 512), f32),
            dma((4,)),
            dma((2,)), dma((2,)),
            dma, dma,
            dma, dma,
            dma((8,)), dma((8,)),
            dma((8,)), dma((8,)),
            dma, dma,
            dma, dma,
            dma, dma,
            dma((2, 8)), dma((4, 4)),
            dma((2, 8)), dma((4, 4)),
            dma((4,)), dma((4,)),
            dma((4,)), dma((4,)),
            dma((8,)), dma((8,)),
            dma((4,)),
        ],
        compiler_params=pltpu.CompilerParams(
            collective_id=0, has_side_effects=True, vmem_limit_bytes=56 * 1024 * 1024
        ),
        cost_estimate=pl.CostEstimate(flops=14_000_000_000, bytes_accessed=9_000_000, transcendentals=500_000),
        name="window",
    )(
        video.reshape(4, 512, 128),
        frame_counts,
        first_weight.reshape(9, 768, 256),
        second_weight,
        cotangent.reshape(8, 64, 512),
    )
    return (
        out[0].reshape(1, 8, 2, 32, 512),
        out[1].reshape(1, 4, 16, 32, 128),
        out[2],
        out[3],
    )


def solution(mesh):
    placed = (
        P("rep", "tm", None, None, None),
        P("rep"),
        P(),
        P(),
        P("rep", None, "tm", None, None),
    )
    return jax.shard_map(
        body,
        mesh=mesh,
        in_specs=placed,
        out_specs=(
            P("rep", None, "tm", None, None),
            P("rep", "tm", None, None, None),
            P("rep", None),
            P("rep", None),
        ),
        check_vma=False,
    )
```

```python
import functools
import math

import jax
import jax.numpy as jnp
from jax import lax
from jax.experimental import pallas as pl
from jax.experimental.pallas import tpu as pltpu
from jax.sharding import PartitionSpec as P

root_half = 0.7071067811865476
MESH = pl.DeviceIdType.MESH
bf16 = jnp.bfloat16
f32 = jnp.float32

NY, NZ, NX = 4, 4, 4
ROWS_F, ROWS_S = 432, 96


def dot(a, b):
    return jnp.dot(a, b, preferred_element_type=f32)


def dot_nt(a, b):
    return lax.dot_general(a, b, (((1,), (1,)), ((), ())), preferred_element_type=f32)


def repeat(count, step):
    def run(i, carry):
        step(i)
        return carry

    lax.fori_loop(0, count, run, 0)


def put_shifted(dst, frame, rows, value, flip):
    lanes = (512, 0) if flip else (0, 512)
    wide = value.astype(f32)
    column = lax.broadcasted_iota(jnp.int32, wide.shape, 1)
    before = jnp.where(column == 0, 0.0, pltpu.roll(wide, 1, 1)).astype(bf16)
    after = jnp.where(column == 31, 0.0, pltpu.roll(wide, 31, 1)).astype(bf16)
    dst[frame, rows, :, lanes[0] : lanes[0] + 256] = before
    dst[frame, rows, :, 256:512] = value
    dst[frame, rows, :, lanes[1] : lanes[1] + 256] = after


def kernel(
    video, counts, first_w, second_w, cotangent,
    feat_out, input_out, first_sums, second_sums,
    vid, w1, w1t, w2, ctp, cts, ct_t, hown, win, xs, acc, gh, sh,
    gpc, gph, gp_t, gpx, pf, r1a, r1b, s1a, s1b, r2a, r2b, s2, r3, ag,
    px, q1, t1, q2, t2, q3, t3, ags, fout, gsend, gout,
    load_sem, win_s, win_r, ed_s, ed_r, fw_s, fw_r, cts_s, cts_r, sh_s, sh_r,
    gp_s, gp_r, gph_s, gph_r, gi_s, gi_r, f1_s, f1a_r, f1b_r, p2a_s, p2a_r, p2b_s, p2b_r,
    p3_s, p3_r, p4_s, p4_r, q1_s, q1_r, q2_s, q2_r, q3_s, q3_r, q4_s, q4_r, out_sem,
):
    rep = lax.axis_index("rep")
    tm = lax.axis_index("tm")
    y, z = rep // NZ, rep % NZ
    x, c = tm // 2, tm % 2

    def remote(src, dst, send, recv, to):
        return pltpu.make_async_remote_copy(
            src_ref=src, dst_ref=dst, send_sem=send, recv_sem=recv, device_id=to, device_id_type=MESH
        )

    def device(to_x, to_y, to_z, to_c):
        return (to_y * NZ + to_z, to_x * 2 + to_c)

    sibling = (rep, x * 2 + 1 - c)

    loads = [
        pltpu.make_async_copy(video, vid, load_sem.at[0]),
        pltpu.make_async_copy(cotangent, ctp.at[pl.ds(0, 8)], load_sem.at[1]),
        pltpu.make_async_copy(second_w, w2, load_sem.at[2]),
        pltpu.make_async_copy(first_w, w1, load_sem.at[3]),
    ]
    for load in loads:
        load.start()

    barrier = pltpu.get_barrier_semaphore()

    def greet(to):
        pl.semaphore_signal(barrier, inc=1, device_id=to, device_id_type=MESH)

    repeat(7, lambda i: greet((rep, (tm + 1 + i) % 8)))
    repeat(3, lambda i: greet(device(x, (y + 1 + i) % NY, z, c)))
    repeat(3, lambda i: greet(device(x, y, (z + 1 + i) % NZ, c)))

    live = counts[0]
    loads[0].wait()

    def keep(frame):
        return jnp.where(tm * 4 + frame < live, 1.0, 0.0).astype(f32)

    for t in range(2):
        even, odd = keep(2 * t), keep(2 * t + 1)
        hown[t, 0:32] = jnp.zeros((32, 256), bf16)
        hown[t, 544:576] = jnp.zeros((32, 256), bf16)

        def pair(n, carry):
            at = pl.ds(pl.multiple_of(n * 64, 64), 64)
            to = pl.ds(pl.multiple_of(n * 64 + 32, 32), 64)
            one = vid[2 * t, at].astype(f32) * even
            two = vid[2 * t + 1, at].astype(f32) * odd
            hown[t, to, 0:128] = ((one + two) * root_half).astype(bf16)
            hown[t, to, 128:256] = ((one - two) * root_half).astype(bf16)
            return carry

        lax.fori_loop(0, 8, pair, 0)

    pl.semaphore_wait(barrier, 13)

    def window_rows(core):
        return pl.ds(pl.multiple_of(96 * core, 32), 96)

    def frames_of(source):
        return pl.ds(2 * source, 2)

    def in_turn(i):
        step = i // 2
        return (x + step + step // 2 - 2 * (step // 3)) % 4 * 2 + (c + i) % 2

    def spread(i):
        to = in_turn((i + 1) % 8)
        rows = pl.ds(pl.multiple_of(32 * (4 * (to // 2) + 3 * (to % 2)), 32), 96)
        return remote(
            hown.at[:, rows],
            win.at[frames_of(tm), window_rows(to % 2)],
            win_s.at[to],
            win_r.at[tm],
            (rep, to),
        )

    repeat(7, lambda i: spread((i + 1) % 7).start())
    win[frames_of(tm), window_rows(c)] = hown[
        :, pl.ds(pl.multiple_of(32 * (4 * x + 3 * c), 32), 96)
    ]

    def edge_rows(core):
        return pl.ds(pl.multiple_of(64 + 32 * core, 32), 32)

    def rest_rows(core):
        return pl.ds(pl.multiple_of(128 * core, 32), 64)

    def hand_edge(source):
        block = win.at[frames_of(source), edge_rows(c)]
        return remote(block, block, ed_s.at[source], ed_r.at[source], sibling)

    def hand_rest(source):
        block = win.at[frames_of(source), rest_rows(c)]
        return remote(block, block, fw_s.at[source], fw_r.at[source], sibling)

    loads[1].wait()
    give_ct = remote(ctp.at[pl.ds(0, 8)], cts, cts_s, cts_r, sibling)
    give_ct.start()

    ctp[8:10] = jnp.zeros((2, 64, 512), bf16)
    loads[2].wait()

    def back_step(n, carry):
        grad = jnp.zeros((256, 512), f32)
        for a in range(3):
            grad = grad + dot_nt(ctp[pl.ds(4 * n + 2 - a, 4)].reshape(256, 512), w2[a])
        low, high = grad[:, :256], grad[:, 256:]
        gh[pl.ds(4 * n, 4), 0] = ((low + high) * root_half).astype(bf16).reshape(4, 64, 256)
        gh[pl.ds(4 * n, 4), 1] = ((low - high) * root_half).astype(bf16).reshape(4, 64, 256)
        return carry

    lax.fori_loop(0, 2, back_step, 0)

    loads[3].wait()

    def turn_tap(n, carry):
        for d in range(3):
            w1t[n, 256 * d : 256 * d + 256] = w1[n, 256 * d : 256 * d + 256].T
        return carry

    lax.fori_loop(0, 9, turn_tap, 0)
    ct_t[:, 0:512] = ctp[0:8].reshape(512, 512).T
    xs[0:2] = jnp.zeros((2, 6, 32, 768), bf16)
    gpx[16:18] = jnp.zeros((2, 4, 32, 768), bf16)
    for j in range(2):
        sh[j, 0:2] = jnp.zeros((2, 64, 512), bf16)
    acc[...] = jnp.zeros_like(acc)

    def take(source, row, count):
        for t in range(2):
            frame = 2 * source + t
            block = win[frame, pl.ds(pl.multiple_of(32 * row, 32), 32 * count)]
            put_shifted(xs, 2 + frame, pl.ds(row, count), block.reshape(count, 32, 256), False)

    def from_afar(i):
        source = in_turn(i)

        @pl.when(source != tm)
        def _():
            block = win.at[frames_of(source), window_rows(c)]
            remote(block, block, win_r.at[source], win_r.at[source], sibling).wait_recv()

        hand_edge(source).start()
        take(source, 3 * c, 3)

    def from_sibling(i):
        source = in_turn(i)
        hand_rest(source).start()
        block = win.at[frames_of(source), edge_rows(1 - c)]
        remote(block, block, ed_r.at[source], ed_r.at[source], sibling).wait_recv()
        take(source, 3 - c, 1)

    repeat(8, from_afar)
    repeat(8, from_sibling)

    def taps(n, carry):
        a, b = n // 3, n % 3
        acc[...] += dot(xs[pl.ds(a, 16), pl.ds(2 * c + b, 2)].reshape(1024, 768), w1[n])
        return carry

    lax.fori_loop(0, 9, taps, 0, unroll=9)

    def activate(n, carry):
        hidden = []
        for t in range(2):
            value = acc[pl.ds(pl.multiple_of(n * 128 + 64 * t, 64), 64)]
            gate = jax.nn.sigmoid(value)
            hidden.append((value * gate).astype(bf16).astype(f32))
            grad = gh[n, t].astype(f32) * (gate * (1.0 + value * (1.0 - gate)))
            gpc[2 * n + t, pl.ds(2 * c, 2)] = grad.astype(bf16).reshape(2, 32, 256)
        sh[0, 2 + n, :, 0:256] = ((hidden[0] + hidden[1]) * root_half).astype(bf16)
        sh[0, 2 + n, :, 256:512] = ((hidden[0] - hidden[1]) * root_half).astype(bf16)
        return carry

    lax.fori_loop(0, 8, activate, 0)
    own_rows = gpc.at[:, pl.ds(2 * c, 2)]
    give_gp = remote(own_rows, own_rows, gp_s, gp_r, sibling)
    give_gp.start()
    give_sh = remote(sh.at[0, pl.ds(2, 8)], sh.at[1, pl.ds(2, 8)], sh_s, sh_r, sibling)
    give_sh.start()
    give_gph = remote(gpc.at[:, 3 * c], gph, gph_s, gph_r, (rep, (tm + 7 + 2 * c) % 8))
    give_gph.start()

    def turn_rows(core):
        at = pl.ds(pl.multiple_of(core * 1024, 1024), 1024)
        gp_t[:, at] = gpc[:, pl.ds(2 * core, 2)].reshape(1024, 256).T

    turn_rows(c)

    def forward(n):
        value = jnp.zeros((256, 512), f32)
        for a in range(3):
            value = value + dot(sh[0, pl.ds(4 * n + a, 4)].reshape(256, 512), w2[a])
        fout[pl.ds(4 * n, 4)] = value.astype(bf16).reshape(4, 64, 512)

    repeat(2, forward)
    write_feat = pltpu.make_async_copy(fout, feat_out, out_sem.at[0])
    write_feat.start()

    def deliver(source, shard):
        to_y, to_z = 2 * c + shard // 4, shard % 4
        stops = (
            (0, r1a.at[y, to_z], device(x, to_y, z, c), f1a_r.at[y, to_z], to_y == y),
            (1, r1b.at[z, shard // 4], device(x, y, to_z, c), f1b_r.at[z, shard // 4], to_z == z),
        )
        for half, slot, to, sem, here in stops:

            @pl.when(here)
            def _(half=half, slot=slot, sem=sem):
                pltpu.make_async_copy(source(half, shard), slot, sem).start()

            @pl.when(jnp.logical_not(here))
            def _(half=half, slot=slot, sem=sem, to=to):
                remote(source(half, shard), slot, f1_s.at[half, shard], sem, to).start()

    def delivered(source, shard):
        to_y, to_z = 2 * c + shard // 4, shard % 4
        for half, here in ((0, to_y == y), (1, to_z == z)):

            @pl.when(jnp.logical_not(here))
            def _(half=half):
                remote(
                    source(half, shard), r1a.at[0, 0], f1_s.at[half, shard], f1_s.at[half, shard], sibling
                ).wait_send()

    def source_f(half, shard):
        return pf.at[half, pl.ds(pl.multiple_of(128 + ROWS_F * shard, 16), ROWS_F)]

    give_gp.wait_recv()
    turn_rows(1 - c)

    def rest_from_sibling(source):
        block = win.at[frames_of(source), rest_rows(1 - c)]
        remote(block, block, fw_r.at[source], fw_r.at[source], sibling).wait_recv()
        take(source, 4 - 4 * c, 2)

    repeat(8, rest_from_sibling)

    def tap(j):
        k = 13 * c + j
        a, b, d = k // 9, (k // 3) % 3, k % 3
        lanes = pl.ds(pl.multiple_of(d * 256, 256), 256)
        upper = xs[pl.ds(a, 16), pl.ds(b, 2), :, lanes].reshape(1024, 256)
        lower = xs[pl.ds(a, 16), pl.ds(b + 2, 2), :, lanes].reshape(1024, 256)
        turned = (dot(gp_t[:, 0:1024], upper) + dot(gp_t[:, 1024:2048], lower)).T.astype(bf16)
        at = pl.ds(pl.multiple_of(256 * j + 128 - 128 * c, 128), 256)
        pf[0, at] = turned[:, :128]
        pf[1, at] = turned[:, 128:]

    odd_row = y % 2

    def send_shards(low):
        repeat(4, lambda k: deliver(source_f, 4 * low + (z + 1 + k) % 4))

    def first_taps(i, carry):
        tap(6 * odd_row + i)
        return carry

    lax.fori_loop(0, 8, first_taps, 0, unroll=4)
    send_shards(odd_row)

    give_ct.wait_recv()
    ct_t[:, 512:1024] = cts[...].reshape(512, 512).T
    give_sh.wait_recv()

    def stop_x(n, k):
        to = (x + k) % 4
        at = pl.ds(pl.multiple_of(256 * n, 256), 256)
        return remote(px.at[to, at], q1.at[x, at], q1_s.at[n, to], q1_r.at[n, x], (rep, 2 * to + c))

    def second_rows(n):
        m = 3 * c + n
        a, band = m // 2, m % 2
        lanes = pl.ds(pl.multiple_of(band * 256, 256), 256)
        own = sh[0, pl.ds(a, 8), :, lanes].reshape(512, 256)
        other = sh[1, pl.ds(a, 8), :, lanes].reshape(512, 256)
        turned = (dot(ct_t[:, 0:512], own) + dot(ct_t[:, 512:1024], other)).T.astype(bf16)
        at = pl.ds(pl.multiple_of(256 * n, 256), 256)
        for to_x in range(4):
            px[to_x, at] = turned[:, 128 * to_x : 128 * to_x + 128]
        repeat(3, lambda k: stop_x(n, k + 1).start())

    repeat(3, second_rows)
    q1[x] = px[x]

    def last_taps(i, carry):
        tap(8 - 8 * odd_row + i)
        return carry

    lax.fori_loop(0, 6, last_taps, 0, unroll=3)
    send_shards(1 - odd_row)

    give_gph.wait_recv()
    inner = jnp.where((c == 0) & (x == 0) | (c == 1) & (x == 3), 0.0, 1.0).astype(bf16)

    def widen(frame, carry):
        put_shifted(gpx, frame, pl.ds(1 - c, 3), gpc[frame, pl.ds(c, 3)], True)
        put_shifted(gpx, frame, pl.ds(3 * c, 1), gph[pl.ds(frame, 1)] * inner, True)
        return carry

    lax.fori_loop(0, 16, widen, 0)
    acc[...] = jnp.zeros_like(acc)

    def input_taps(n, carry):
        a, b = n // 3, n % 3
        acc[...] += dot(gpx[pl.ds(2 - a, 16), pl.ds(2 - b, 2)].reshape(1024, 768), w1t[n])
        return carry

    lax.fori_loop(0, 9, input_taps, 0, unroll=3)

    def unpair(n, carry):
        for t in range(2):
            at = pl.ds(pl.multiple_of(n * 128 + 64 * t, 64), 64)
            low, high = acc[at, 0:128], acc[at, 128:256]
            even = jnp.where(4 * n + 2 * t < live, 1.0, 0.0).astype(f32)
            odd = jnp.where(4 * n + 2 * t + 1 < live, 1.0, 0.0).astype(f32)
            gsend[n, 2 * t] = ((low + high) * root_half * even).astype(bf16)
            gsend[n, 2 * t + 1] = ((low - high) * root_half * odd).astype(bf16)
        return carry

    lax.fori_loop(0, 8, unpair, 0)

    def pixel_rows(source):
        return gout.at[:, pl.ds(pl.multiple_of(64 * source, 64), 64)]

    def give_back(i):
        to = in_turn(i + 1)
        return remote(gsend.at[to], pixel_rows(tm), gi_s.at[to], gi_r.at[tm], (rep, to))

    repeat(7, lambda i: give_back(6 - i).start())
    gout[:, pl.ds(pl.multiple_of(64 * tm, 64), 64)] = gsend[tm]

    owner = c == y // 2

    def peer_of(i, home):
        return (home + 1 + i) % 4

    def wait_for(slot, sem):
        remote(slot, slot, sem, sem, sibling).wait_recv()

    def from_x(i):
        n, peer = i // 3, peer_of(i % 3, x)
        wait_for(q1.at[peer, pl.ds(pl.multiple_of(256 * n, 256), 256)], q1_r.at[n, peer])

    repeat(9, from_x)

    def four(ref, *index):
        total = ref[(0,) + index].astype(f32)
        for source in range(1, 4):
            total = total + ref[(source,) + index].astype(f32)
        return total.astype(bf16)

    def sum_x(i, carry):
        t1[i] = four(q1, pl.ds(pl.multiple_of(96 * i, 16), 96))
        return carry

    lax.fori_loop(0, 8, sum_x, 0)

    def give_y(i):
        return remote(
            t1.at[pl.ds(4 * i, 4)], q2.at[y], q2_s.at[i], q2_r.at[y], device(x, 2 * c + i, z, c)
        )

    def start_y(i):
        @pl.when(2 * c + i != y)
        def _():
            give_y(i).start()

        @pl.when(2 * c + i == y)
        def _():
            q2[y] = t1[pl.ds(4 * i, 4)]

    repeat(2, start_y)

    def landed(slot, sem):
        pltpu.make_async_copy(slot, slot, sem).wait()

    def give_b(i):
        return remote(s1b.at[i], r2b.at[y], p2b_s.at[i], p2b_r.at[y], device(x, 2 * c + i, z, c))

    def give_a(k):
        return remote(s1a.at[k], r2a.at[z], p2a_s.at[k], p2a_r.at[z], device(x, y, k, c))

    def give_z(k):
        return remote(t2.at[k], q3.at[z], q3_s.at[k], q3_r.at[z], device(x, y, k, c))

    def sum_b(i):
        repeat(4, lambda source: landed(r1b.at[source, i], f1b_r.at[source, i]))
        s1b[i] = four(r1b, i)

        @pl.when(2 * c + i != y)
        def _():
            give_b(i).start()

        @pl.when(2 * c + i == y)
        def _():
            r2b[y] = s1b[i]

    sum_b(odd_row)

    @pl.when(owner)
    def _():
        def sum_a(k):
            repeat(4, lambda source: landed(r1a.at[source, k], f1a_r.at[source, k]))
            s1a[k] = four(r1a, k)

            @pl.when(k != z)
            def _():
                give_a(k).start()

        repeat(4, lambda k: sum_a((z + 1 + k) % 4))
        r2a[z] = s1a[z]

    sum_b(1 - odd_row)

    @pl.when(owner)
    def _():
        repeat(3, lambda i: wait_for(q2.at[peer_of(i, y)], q2_r.at[peer_of(i, y)]))

        def sum_y(k):
            t2[k] = four(q2, k)

            @pl.when(k != z)
            def _():
                give_z(k).start()

        repeat(4, lambda k: sum_y((z + 1 + k) % 4))
        q3[z] = t2[z]

    def give_x(k):
        return remote(s2, r3.at[x], p3_s.at[k], p3_r.at[x], (rep, (x + k) % 4 * 2 + c))

    def give_second(k):
        return remote(t3, ags.at[x], q4_s.at[k], q4_r.at[x], (rep, (tm + k) % 8))

    give_first = remote(ag, ag, p4_s, p4_r, sibling)
    @pl.when(owner)
    def _():
        repeat(3, lambda i: wait_for(r2a.at[peer_of(i, z)], p2a_r.at[peer_of(i, z)]))
        repeat(3, lambda i: wait_for(r2b.at[peer_of(i, y)], p2b_r.at[peer_of(i, y)]))
        s2[0] = four(r2a)
        s2[1] = four(r2b)
        repeat(3, lambda i: give_x(i + 1).start())
        r3[x] = s2[...]
        repeat(3, lambda i: wait_for(q3.at[peer_of(i, z)], q3_r.at[peer_of(i, z)]))
        t3[...] = four(q3)
        repeat(7, lambda i: give_second(i + 1).start())
        ags[x] = t3[...]
        repeat(3, lambda i: wait_for(r3.at[peer_of(i, x)], p3_r.at[peer_of(i, x)]))

        def sum_half(half):
            ag[half] = four(r3, half)

        repeat(2, sum_half)
        give_first.start()

    @pl.when(jnp.logical_not(owner))
    def _():
        give_first.wait_recv()

    write_first = pltpu.make_async_copy(ag, first_sums, out_sem.at[2])
    write_first.start()
    def from_rows(i):
        source = in_turn((tm + 1 + i) % 8)

        @pl.when(source != tm)
        def _():
            wait_for(pixel_rows(source), gi_r.at[source])

    repeat(8, from_rows)
    write_input = pltpu.make_async_copy(gout, input_out, out_sem.at[1])
    write_input.start()

    def take_sums(peer):
        @pl.when(jnp.logical_not(owner) | (peer != x))
        def _():
            wait_for(ags.at[peer], q4_r.at[peer])

    repeat(4, take_sums)

    write_second = pltpu.make_async_copy(ags, second_sums, out_sem.at[3])
    write_second.start()
    for copy in [give_ct, give_gp, give_sh, give_gph]:
        copy.wait_send()
    repeat(7, lambda i: spread(i).wait_send())
    repeat(7, lambda i: give_back(i).wait_send())
    repeat(9, lambda i: stop_x(i // 3, i % 3 + 1).wait_send())

    def drain_hand(source):
        hand_edge(source).wait_send()
        hand_rest(source).wait_send()

    repeat(8, drain_hand)

    def drain(shard, carry):
        delivered(source_f, shard)
        return carry

    lax.fori_loop(0, 8, drain, 0)

    def drain_y(i):
        @pl.when(2 * c + i != y)
        def _():
            give_y(i).wait_send()
            give_b(i).wait_send()

    repeat(2, drain_y)

    @pl.when(owner)
    def _():
        def drain_z(i):
            k = peer_of(i, z)
            give_a(k).wait_send()
            give_z(k).wait_send()
            give_x(i + 1).wait_send()

        repeat(3, drain_z)
        repeat(7, lambda i: give_second(i + 1).wait_send())
        give_first.wait_send()

    for write in (write_feat, write_input, write_first, write_second):
        write.wait()


def finish(features, grad_input, first, second, feat_out, input_out, first_out, second_out):
    feat_out[...] = features[...]
    input_out[...] = grad_input[...]
    scale_first = 1.0 / math.sqrt(131072)
    scale_second = 1.0 / math.sqrt(65536)
    for half in range(2):
        first_out[:, 128 * half : 128 * half + 128] = first[half].astype(f32) * scale_first
    for quarter in range(4):
        second_out[:, 128 * quarter : 128 * quarter + 128] = second[quarter].astype(f32) * scale_second


def body(video, frame_counts, first_weight, second_weight, cotangent):
    any_ = pl.BlockSpec(memory_space=pl.ANY)
    vmem = pltpu.VMEM
    dma = pltpu.SemaphoreType.DMA
    features, grad_input, first, second = pl.pallas_call(
        kernel,
        out_shape=(
            jax.ShapeDtypeStruct((8, 64, 512), bf16),
            jax.ShapeDtypeStruct((4, 512, 128), bf16),
            jax.ShapeDtypeStruct((2, ROWS_F, 128), bf16),
            jax.ShapeDtypeStruct((4, ROWS_S, 128), bf16),
        ),
        in_specs=[any_, pl.BlockSpec(memory_space=pltpu.SMEM), any_, any_, any_],
        out_specs=(any_,) * 4,
        scratch_shapes=[
            vmem((4, 512, 128), bf16),
            vmem((9, 768, 256), bf16),
            vmem((9, 768, 256), bf16),
            vmem((3, 512, 512), bf16),
            vmem((10, 64, 512), bf16),
            vmem((8, 64, 512), bf16),
            vmem((512, 1024), bf16),
            vmem((2, 576, 256), bf16),
            vmem((16, 192, 256), bf16),
            vmem((18, 6, 32, 768), bf16),
            vmem((1024, 256), f32),
            vmem((8, 2, 64, 256), bf16),
            vmem((2, 10, 64, 512), bf16),
            vmem((16, 4, 32, 256), bf16),
            vmem((16, 32, 256), bf16),
            vmem((256, 2048), bf16),
            vmem((18, 4, 32, 768), bf16),
            vmem((2, 3712, 128), bf16),
            vmem((4, 4, ROWS_F, 128), bf16),
            vmem((4, 2, ROWS_F, 128), bf16),
            vmem((4, ROWS_F, 128), bf16),
            vmem((2, ROWS_F, 128), bf16),
            vmem((4, ROWS_F, 128), bf16),
            vmem((4, ROWS_F, 128), bf16),
            vmem((2, ROWS_F, 128), bf16),
            vmem((4, 2, ROWS_F, 128), bf16),
            vmem((2, ROWS_F, 128), bf16),
            vmem((4, 768, 128), bf16),
            vmem((4, 768, 128), bf16),
            vmem((8, ROWS_S, 128), bf16),
            vmem((4, 4, ROWS_S, 128), bf16),
            vmem((4, ROWS_S, 128), bf16),
            vmem((4, ROWS_S, 128), bf16),
            vmem((ROWS_S, 128), bf16),
            vmem((4, ROWS_S, 128), bf16),
            vmem((8, 64, 512), bf16),
            vmem((8, 4, 64, 128), bf16),
            vmem((4, 512, 128), bf16),
            dma((4,)),
            dma((8,)), dma((8,)),
            dma((8,)), dma((8,)),
            dma((8,)), dma((8,)),
            dma, dma,
            dma, dma,
            dma, dma,
            dma, dma,
            dma((8,)), dma((8,)),
            dma((2, 8)), dma((4, 4)), dma((4, 2)),
            dma((4,)), dma((4,)), dma((2,)), dma((4,)),
            dma((4,)), dma((4,)),
            dma, dma,
            dma((3, 4)), dma((3, 4)),
            dma((2,)), dma((4,)),
            dma((4,)), dma((4,)),
            dma((8,)), dma((4,)),
            dma((4,)),
        ],
        compiler_params=pltpu.CompilerParams(
            collective_id=0, has_side_effects=True, vmem_limit_bytes=56 * 1024 * 1024
        ),
        cost_estimate=pl.CostEstimate(flops=14_000_000_000, bytes_accessed=9_000_000, transcendentals=500_000),
        name="window",
    )(
        video.reshape(4, 512, 128),
        frame_counts,
        first_weight.reshape(9, 768, 256),
        second_weight,
        cotangent.reshape(8, 64, 512),
    )
    features, grad_input, grad_first, grad_second = pl.pallas_call(
        finish,
        out_shape=(
            jax.ShapeDtypeStruct((8, 64, 512), bf16),
            jax.ShapeDtypeStruct((4, 512, 128), bf16),
            jax.ShapeDtypeStruct((432, 256), f32),
            jax.ShapeDtypeStruct((96, 512), f32),
        ),
        name="finish",
    )(features, grad_input, first, second)
    return (
        features.reshape(1, 8, 2, 32, 512),
        grad_input.reshape(1, 4, 16, 32, 128),
        grad_first,
        grad_second,
    )


def solution(mesh):
    placed = (
        P("rep", "tm", None, None, None),
        P("rep"),
        P(),
        P(),
        P("rep", None, "tm", None, None),
    )
    return jax.shard_map(
        body,
        mesh=mesh,
        in_specs=placed,
        out_specs=(
            P("rep", None, "tm", None, None),
            P("rep", "tm", None, None, None),
            P("rep", None),
            P("rep", None),
        ),
        check_vma=False,
    )
```

```python
import functools
import math

import jax
import jax.numpy as jnp
from jax import lax
from jax.experimental import pallas as pl
from jax.experimental.pallas import tpu as pltpu
from jax.sharding import PartitionSpec as P

root_half = 0.7071067811865476
MESH = pl.DeviceIdType.MESH
bf16 = jnp.bfloat16
f32 = jnp.float32

NY, NZ, NX = 4, 4, 4
ROWS_F, ROWS_S = 432, 96


def dot(a, b):
    return jnp.dot(a, b, preferred_element_type=f32)


def dot_nt(a, b):
    return lax.dot_general(a, b, (((1,), (1,)), ((), ())), preferred_element_type=f32)


def repeat(count, step):
    def run(i, carry):
        step(i)
        return carry

    lax.fori_loop(0, count, run, 0)


def put_shifted(dst, frame, rows, value, flip):
    lanes = (512, 0) if flip else (0, 512)
    wide = value.astype(f32)
    column = lax.broadcasted_iota(jnp.int32, wide.shape, 1)
    before = jnp.where(column == 0, 0.0, pltpu.roll(wide, 1, 1)).astype(bf16)
    after = jnp.where(column == 31, 0.0, pltpu.roll(wide, 31, 1)).astype(bf16)
    dst[frame, rows, :, lanes[0] : lanes[0] + 256] = before
    dst[frame, rows, :, 256:512] = value
    dst[frame, rows, :, lanes[1] : lanes[1] + 256] = after


def kernel(
    video, counts, first_w, second_w, cotangent,
    feat_out, input_out, first_sums, second_sums,
    vid, w1, w1t, w2, ctp, cts, ct_t, hown, win, xs, acc, gh, sh,
    gpc, gph, gp_t, gpx, pf, r1a, r1b, s1a, s1b, r2a, r2b, s2, r3, ag,
    px, q1, t1, q2, t2, q3, t3, ags, fout, gsend, gout,
    load_sem, win_s, win_r, ed_s, ed_r, fw_s, fw_r, cts_s, cts_r, sh_s, sh_r,
    gp_s, gp_r, gph_s, gph_r, gi_s, gi_r, f1_s, f1a_r, f1b_r, p2a_s, p2a_r, p2b_s, p2b_r,
    p3_s, p3_r, p4_s, p4_r, q1_s, q1_r, q2_s, q2_r, q3_s, q3_r, q4_s, q4_r, out_sem,
):
    rep = lax.axis_index("rep")
    tm = lax.axis_index("tm")
    y, z = rep // NZ, rep % NZ
    x, c = tm // 2, tm % 2

    def remote(src, dst, send, recv, to):
        return pltpu.make_async_remote_copy(
            src_ref=src, dst_ref=dst, send_sem=send, recv_sem=recv, device_id=to, device_id_type=MESH
        )

    def device(to_x, to_y, to_z, to_c):
        return (to_y * NZ + to_z, to_x * 2 + to_c)

    sibling = (rep, x * 2 + 1 - c)

    loads = [
        pltpu.make_async_copy(video, vid, load_sem.at[0]),
        pltpu.make_async_copy(cotangent, ctp.at[pl.ds(0, 8)], load_sem.at[1]),
        pltpu.make_async_copy(second_w, w2, load_sem.at[2]),
        pltpu.make_async_copy(first_w, w1, load_sem.at[3]),
    ]
    barrier = pltpu.get_barrier_semaphore()

    def greet(to):
        pl.semaphore_signal(barrier, inc=1, device_id=to, device_id_type=MESH)

    repeat(7, lambda i: greet((rep, (tm + 1 + i) % 8)))
    repeat(3, lambda i: greet(device(x, (y + 1 + i) % NY, z, c)))
    repeat(3, lambda i: greet(device(x, y, (z + 1 + i) % NZ, c)))

    for load in loads:
        load.start()

    live = counts[0]
    loads[0].wait()

    def keep(frame):
        return jnp.where(tm * 4 + frame < live, 1.0, 0.0).astype(f32)

    for t in range(2):
        even, odd = keep(2 * t), keep(2 * t + 1)
        hown[t, 0:32] = jnp.zeros((32, 256), bf16)
        hown[t, 544:576] = jnp.zeros((32, 256), bf16)

        def pair(n, carry):
            at = pl.ds(pl.multiple_of(n * 64, 64), 64)
            to = pl.ds(pl.multiple_of(n * 64 + 32, 32), 64)
            one = vid[2 * t, at].astype(f32) * even
            two = vid[2 * t + 1, at].astype(f32) * odd
            hown[t, to, 0:128] = ((one + two) * root_half).astype(bf16)
            hown[t, to, 128:256] = ((one - two) * root_half).astype(bf16)
            return carry

        lax.fori_loop(0, 8, pair, 0)

    pl.semaphore_wait(barrier, 13)

    def window_rows(core):
        return pl.ds(pl.multiple_of(96 * core, 32), 96)

    def frames_of(source):
        return pl.ds(2 * source, 2)

    def in_turn(i):
        step = i // 2
        return (x + step + step // 2 - 2 * (step // 3)) % 4 * 2 + (c + i) % 2

    def spread(i):
        to = in_turn((i + 1) % 8)
        rows = pl.ds(pl.multiple_of(32 * (4 * (to // 2) + 3 * (to % 2)), 32), 96)
        return remote(
            hown.at[:, rows],
            win.at[frames_of(tm), window_rows(to % 2)],
            win_s.at[to],
            win_r.at[tm],
            (rep, to),
        )

    repeat(7, lambda i: spread((i + 1) % 7).start())
    win[frames_of(tm), window_rows(c)] = hown[
        :, pl.ds(pl.multiple_of(32 * (4 * x + 3 * c), 32), 96)
    ]

    def edge_rows(core):
        return pl.ds(pl.multiple_of(64 + 32 * core, 32), 32)

    def rest_rows(core):
        return pl.ds(pl.multiple_of(128 * core, 32), 64)

    def hand_edge(source):
        block = win.at[frames_of(source), edge_rows(c)]
        return remote(block, block, ed_s.at[source], ed_r.at[source], sibling)

    def hand_rest(source):
        block = win.at[frames_of(source), rest_rows(c)]
        return remote(block, block, fw_s.at[source], fw_r.at[source], sibling)

    loads[1].wait()
    give_ct = remote(ctp.at[pl.ds(0, 8)], cts, cts_s, cts_r, sibling)
    give_ct.start()

    ctp[8:10] = jnp.zeros((2, 64, 512), bf16)
    loads[2].wait()

    def back_step(n, carry):
        grad = jnp.zeros((256, 512), f32)
        for a in range(3):
            grad = grad + dot_nt(ctp[pl.ds(4 * n + 2 - a, 4)].reshape(256, 512), w2[a])
        low, high = grad[:, :256], grad[:, 256:]
        gh[pl.ds(4 * n, 4), 0] = ((low + high) * root_half).astype(bf16).reshape(4, 64, 256)
        gh[pl.ds(4 * n, 4), 1] = ((low - high) * root_half).astype(bf16).reshape(4, 64, 256)
        return carry

    lax.fori_loop(0, 2, back_step, 0)

    loads[3].wait()

    def turn_tap(n, carry):
        for d in range(3):
            w1t[n, 256 * d : 256 * d + 256] = w1[n, 256 * d : 256 * d + 256].T
        return carry

    lax.fori_loop(0, 9, turn_tap, 0)
    ct_t[:, 0:512] = ctp[0:8].reshape(512, 512).T
    xs[0:2] = jnp.zeros((2, 6, 32, 768), bf16)
    gpx[16:18] = jnp.zeros((2, 4, 32, 768), bf16)
    for j in range(2):
        sh[j, 0:2] = jnp.zeros((2, 64, 512), bf16)
    acc[...] = jnp.zeros_like(acc)

    def take(source, row, count):
        for t in range(2):
            frame = 2 * source + t
            block = win[frame, pl.ds(pl.multiple_of(32 * row, 32), 32 * count)]
            put_shifted(xs, 2 + frame, pl.ds(row, count), block.reshape(count, 32, 256), False)

    def from_afar(i):
        source = in_turn(i)

        @pl.when(source != tm)
        def _():
            block = win.at[frames_of(source), window_rows(c)]
            remote(block, block, win_r.at[source], win_r.at[source], sibling).wait_recv()

        hand_edge(source).start()
        take(source, 3 * c, 3)

    def from_sibling(i):
        source = in_turn(i)
        hand_rest(source).start()
        block = win.at[frames_of(source), edge_rows(1 - c)]
        remote(block, block, ed_r.at[source], ed_r.at[source], sibling).wait_recv()
        take(source, 3 - c, 1)

    repeat(8, from_afar)
    repeat(8, from_sibling)

    def taps(n, carry):
        a, b = n // 3, n % 3
        acc[...] += dot(xs[pl.ds(a, 16), pl.ds(2 * c + b, 2)].reshape(1024, 768), w1[n])
        return carry

    lax.fori_loop(0, 9, taps, 0, unroll=9)

    def activate(n, carry):
        hidden = []
        for t in range(2):
            value = acc[pl.ds(pl.multiple_of(n * 128 + 64 * t, 64), 64)]
            gate = jax.nn.sigmoid(value)
            hidden.append((value * gate).astype(bf16).astype(f32))
            grad = gh[n, t].astype(f32) * (gate * (1.0 + value * (1.0 - gate)))
            gpc[2 * n + t, pl.ds(2 * c, 2)] = grad.astype(bf16).reshape(2, 32, 256)
        sh[0, 2 + n, :, 0:256] = ((hidden[0] + hidden[1]) * root_half).astype(bf16)
        sh[0, 2 + n, :, 256:512] = ((hidden[0] - hidden[1]) * root_half).astype(bf16)
        return carry

    lax.fori_loop(0, 8, activate, 0)
    own_rows = gpc.at[:, pl.ds(2 * c, 2)]
    give_gp = remote(own_rows, own_rows, gp_s, gp_r, sibling)
    give_gp.start()
    give_sh = remote(sh.at[0, pl.ds(2, 8)], sh.at[1, pl.ds(2, 8)], sh_s, sh_r, sibling)
    give_sh.start()
    give_gph = remote(gpc.at[:, 3 * c], gph, gph_s, gph_r, (rep, (tm + 7 + 2 * c) % 8))
    give_gph.start()

    def turn_rows(core):
        at = pl.ds(pl.multiple_of(core * 1024, 1024), 1024)
        gp_t[:, at] = gpc[:, pl.ds(2 * core, 2)].reshape(1024, 256).T

    turn_rows(c)

    def forward(n):
        value = jnp.zeros((256, 512), f32)
        for a in range(3):
            value = value + dot(sh[0, pl.ds(4 * n + a, 4)].reshape(256, 512), w2[a])
        fout[pl.ds(4 * n, 4)] = value.astype(bf16).reshape(4, 64, 512)

    repeat(2, forward)
    write_feat = pltpu.make_async_copy(fout, feat_out, out_sem.at[0])
    write_feat.start()

    def deliver(source, shard):
        to_y, to_z = 2 * c + shard // 4, shard % 4
        stops = (
            (0, r1a.at[y, to_z], device(x, to_y, z, c), f1a_r.at[y, to_z], to_y == y),
            (1, r1b.at[z, shard // 4], device(x, y, to_z, c), f1b_r.at[z, shard // 4], to_z == z),
        )
        for half, slot, to, sem, here in stops:

            @pl.when(here)
            def _(half=half, slot=slot, sem=sem):
                pltpu.make_async_copy(source(half, shard), slot, sem).start()

            @pl.when(jnp.logical_not(here))
            def _(half=half, slot=slot, sem=sem, to=to):
                remote(source(half, shard), slot, f1_s.at[half, shard], sem, to).start()

    def delivered(source, shard):
        to_y, to_z = 2 * c + shard // 4, shard % 4
        for half, here in ((0, to_y == y), (1, to_z == z)):

            @pl.when(jnp.logical_not(here))
            def _(half=half):
                remote(
                    source(half, shard), r1a.at[0, 0], f1_s.at[half, shard], f1_s.at[half, shard], sibling
                ).wait_send()

    def source_f(half, shard):
        return pf.at[half, pl.ds(pl.multiple_of(128 + ROWS_F * shard, 16), ROWS_F)]

    def rest_from_sibling(source):
        block = win.at[frames_of(source), rest_rows(1 - c)]
        remote(block, block, fw_r.at[source], fw_r.at[source], sibling).wait_recv()
        take(source, 4 - 4 * c, 2)

    repeat(8, rest_from_sibling)

    give_gp.wait_recv()
    turn_rows(1 - c)

    def tap(j):
        k = 13 * c + j
        a, b, d = k // 9, (k // 3) % 3, k % 3
        lanes = pl.ds(pl.multiple_of(d * 256, 256), 256)
        upper = xs[pl.ds(a, 16), pl.ds(b, 2), :, lanes].reshape(1024, 256)
        lower = xs[pl.ds(a, 16), pl.ds(b + 2, 2), :, lanes].reshape(1024, 256)
        turned = (dot(gp_t[:, 0:1024], upper) + dot(gp_t[:, 1024:2048], lower)).T.astype(bf16)
        at = pl.ds(pl.multiple_of(256 * j + 128 - 128 * c, 128), 256)
        pf[0, at] = turned[:, :128]
        pf[1, at] = turned[:, 128:]

    odd_row = y % 2

    def in_order(index, last):
        return last * odd_row + (1 - 2 * odd_row) * index

    def send_pair(pair):
        repeat(2, lambda k: deliver(source_f, in_order(2 * pair + (z + k) % 2, 7)))

    def first_taps(n):
        for i in range(4):
            tap(in_order(4 * n + i, 13))
        send_pair(n)

    repeat(2, first_taps)

    give_ct.wait_recv()
    ct_t[:, 512:1024] = cts[...].reshape(512, 512).T
    give_sh.wait_recv()

    def stop_x(n, k):
        to = (x + k) % 4
        at = pl.ds(pl.multiple_of(256 * n, 256), 256)
        return remote(px.at[to, at], q1.at[x, at], q1_s.at[n, to], q1_r.at[n, x], (rep, 2 * to + c))

    def second_rows(n):
        m = 3 * c + n
        a, band = m // 2, m % 2
        lanes = pl.ds(pl.multiple_of(band * 256, 256), 256)
        own = sh[0, pl.ds(a, 8), :, lanes].reshape(512, 256)
        other = sh[1, pl.ds(a, 8), :, lanes].reshape(512, 256)
        turned = (dot(ct_t[:, 0:512], own) + dot(ct_t[:, 512:1024], other)).T.astype(bf16)
        at = pl.ds(pl.multiple_of(256 * n, 256), 256)
        for to_x in range(4):
            px[to_x, at] = turned[:, 128 * to_x : 128 * to_x + 128]
        repeat(3, lambda k: stop_x(n, k + 1).start())

    repeat(3, second_rows)
    q1[x] = px[x]

    def last_taps(n):
        for i in range(3):
            tap(in_order(8 + 3 * n + i, 13))
        send_pair(2 + n)

    repeat(2, last_taps)

    give_gph.wait_recv()
    inner = jnp.where((c == 0) & (x == 0) | (c == 1) & (x == 3), 0.0, 1.0).astype(bf16)

    def widen(frame, carry):
        put_shifted(gpx, frame, pl.ds(1 - c, 3), gpc[frame, pl.ds(c, 3)], True)
        put_shifted(gpx, frame, pl.ds(3 * c, 1), gph[pl.ds(frame, 1)] * inner, True)
        return carry

    lax.fori_loop(0, 16, widen, 0)
    acc[...] = jnp.zeros_like(acc)

    def input_taps(n, carry):
        a, b = n // 3, n % 3
        acc[...] += dot(gpx[pl.ds(2 - a, 16), pl.ds(2 - b, 2)].reshape(1024, 768), w1t[n])
        return carry

    lax.fori_loop(0, 9, input_taps, 0, unroll=3)

    def unpair(n, carry):
        for t in range(2):
            at = pl.ds(pl.multiple_of(n * 128 + 64 * t, 64), 64)
            low, high = acc[at, 0:128], acc[at, 128:256]
            even = jnp.where(4 * n + 2 * t < live, 1.0, 0.0).astype(f32)
            odd = jnp.where(4 * n + 2 * t + 1 < live, 1.0, 0.0).astype(f32)
            gsend[n, 2 * t] = ((low + high) * root_half * even).astype(bf16)
            gsend[n, 2 * t + 1] = ((low - high) * root_half * odd).astype(bf16)
        return carry

    lax.fori_loop(0, 8, unpair, 0)

    def pixel_rows(source):
        return gout.at[:, pl.ds(pl.multiple_of(64 * source, 64), 64)]

    def give_back(i):
        to = in_turn(i + 1)
        return remote(gsend.at[to], pixel_rows(tm), gi_s.at[to], gi_r.at[tm], (rep, to))

    repeat(7, lambda i: give_back(6 - i).start())
    gout[:, pl.ds(pl.multiple_of(64 * tm, 64), 64)] = gsend[tm]

    owner = c == y // 2

    def peer_of(i, home):
        return (home + 1 + i) % 4

    def wait_for(slot, sem):
        remote(slot, slot, sem, sem, sibling).wait_recv()

    def from_x(i):
        n, peer = i // 3, peer_of(i % 3, x)
        wait_for(q1.at[peer, pl.ds(pl.multiple_of(256 * n, 256), 256)], q1_r.at[n, peer])

    repeat(9, from_x)

    def four(ref, *index):
        total = ref[(0,) + index].astype(f32)
        for source in range(1, 4):
            total = total + ref[(source,) + index].astype(f32)
        return total.astype(bf16)

    def sum_x(i, carry):
        t1[i] = four(q1, pl.ds(pl.multiple_of(96 * i, 16), 96))
        return carry

    lax.fori_loop(0, 8, sum_x, 0)

    def give_y(i):
        return remote(
            t1.at[pl.ds(4 * i, 4)], q2.at[y], q2_s.at[i], q2_r.at[y], device(x, 2 * c + i, z, c)
        )

    def start_y(i):
        @pl.when(2 * c + i != y)
        def _():
            give_y(i).start()

        @pl.when(2 * c + i == y)
        def _():
            q2[y] = t1[pl.ds(4 * i, 4)]

    repeat(2, start_y)

    def landed(slot, sem):
        pltpu.make_async_copy(slot, slot, sem).wait()

    def give_b(i):
        return remote(s1b.at[i], r2b.at[y], p2b_s.at[i], p2b_r.at[y], device(x, 2 * c + i, z, c))

    def give_a(k):
        return remote(s1a.at[k], r2a.at[z], p2a_s.at[k], p2a_r.at[z], device(x, y, k, c))

    def give_z(k):
        return remote(t2.at[k], q3.at[z], q3_s.at[k], q3_r.at[z], device(x, y, k, c))

    def sum_b(i):
        repeat(4, lambda source: landed(r1b.at[source, i], f1b_r.at[source, i]))
        s1b[i] = four(r1b, i)

        @pl.when(2 * c + i != y)
        def _():
            give_b(i).start()

        @pl.when(2 * c + i == y)
        def _():
            r2b[y] = s1b[i]

    sum_b(odd_row)

    @pl.when(owner)
    def _():
        def sum_a(k):
            repeat(4, lambda source: landed(r1a.at[source, k], f1a_r.at[source, k]))
            s1a[k] = four(r1a, k)

            @pl.when(k != z)
            def _():
                give_a(k).start()

        repeat(4, lambda k: sum_a((z + 1 + k) % 4))
        r2a[z] = s1a[z]

    sum_b(1 - odd_row)

    @pl.when(owner)
    def _():
        repeat(3, lambda i: wait_for(q2.at[peer_of(i, y)], q2_r.at[peer_of(i, y)]))

        def sum_y(k):
            t2[k] = four(q2, k)

            @pl.when(k != z)
            def _():
                give_z(k).start()

        repeat(4, lambda k: sum_y((z + 1 + k) % 4))
        q3[z] = t2[z]

    def give_x(half, k):
        slot = r3.at[x, half]
        return remote(s2.at[half], slot, p3_s.at[half, k], p3_r.at[half, x], (rep, (x + k) % 4 * 2 + c))

    def give_second(k):
        return remote(t3, ags.at[x], q4_s.at[k], q4_r.at[x], (rep, (tm + k) % 8))

    def give_first(half):
        return remote(ag.at[half], ag.at[half], p4_s.at[half], p4_r.at[half], sibling)

    @pl.when(owner)
    def _():
        for half, slots, sems, home in ((0, r2a, p2a_r, z), (1, r2b, p2b_r, y)):
            repeat(3, lambda i: wait_for(slots.at[peer_of(i, home)], sems.at[peer_of(i, home)]))
            s2[half] = four(slots)
            repeat(3, lambda i: give_x(half, i + 1).start())
        r3[x] = s2[...]
        repeat(3, lambda i: wait_for(q3.at[peer_of(i, z)], q3_r.at[peer_of(i, z)]))
        t3[...] = four(q3)
        repeat(7, lambda i: give_second(i + 1).start())
        ags[x] = t3[...]

    def from_rows(i):
        source = in_turn((tm + 1 + i) % 8)

        @pl.when(source != tm)
        def _():
            wait_for(pixel_rows(source), gi_r.at[source])

    repeat(8, from_rows)
    write_input = pltpu.make_async_copy(gout, input_out, out_sem.at[1])
    write_input.start()

    for copy in [give_ct, give_gp, give_sh, give_gph]:
        copy.wait_send()
    repeat(7, lambda i: spread(i).wait_send())
    repeat(7, lambda i: give_back(i).wait_send())
    repeat(9, lambda i: stop_x(i // 3, i % 3 + 1).wait_send())

    def drain_hand(source):
        hand_edge(source).wait_send()
        hand_rest(source).wait_send()

    repeat(8, drain_hand)
    repeat(8, lambda shard: delivered(source_f, shard))

    def drain_y(i):
        @pl.when(2 * c + i != y)
        def _():
            give_y(i).wait_send()
            give_b(i).wait_send()

    repeat(2, drain_y)

    @pl.when(owner)
    def _():
        def drain_z(i):
            k = peer_of(i, z)
            give_a(k).wait_send()
            give_z(k).wait_send()

        repeat(3, drain_z)
        def sum_half(half):
            repeat(3, lambda i: wait_for(r3.at[peer_of(i, x), half], p3_r.at[half, peer_of(i, x)]))
            ag[half] = four(r3, half)
            give_first(half).start()

        repeat(2, sum_half)

    @pl.when(jnp.logical_not(owner))
    def _():
        repeat(2, lambda half: give_first(half).wait_recv())

    write_first = pltpu.make_async_copy(ag, first_sums, out_sem.at[2])
    write_first.start()

    def take_sums(peer):
        @pl.when(jnp.logical_not(owner) | (peer != x))
        def _():
            wait_for(ags.at[peer], q4_r.at[peer])

    repeat(4, take_sums)
    write_second = pltpu.make_async_copy(ags, second_sums, out_sem.at[3])
    write_second.start()

    @pl.when(owner)
    def _():
        repeat(6, lambda i: give_x(i // 3, i % 3 + 1).wait_send())
        repeat(7, lambda i: give_second(i + 1).wait_send())
        repeat(2, lambda half: give_first(half).wait_send())

    for write in (write_feat, write_input, write_first, write_second):
        write.wait()


def finish(features, grad_input, first, second, feat_out, input_out, first_out, second_out):
    feat_out[...] = features[...]
    input_out[...] = grad_input[...]
    scale_first = 1.0 / math.sqrt(131072)
    scale_second = 1.0 / math.sqrt(65536)
    for half in range(2):
        first_out[:, 128 * half : 128 * half + 128] = first[half].astype(f32) * scale_first
    for quarter in range(4):
        second_out[:, 128 * quarter : 128 * quarter + 128] = second[quarter].astype(f32) * scale_second


def body(video, frame_counts, first_weight, second_weight, cotangent):
    any_ = pl.BlockSpec(memory_space=pl.ANY)
    vmem = pltpu.VMEM
    dma = pltpu.SemaphoreType.DMA
    features, grad_input, first, second = pl.pallas_call(
        kernel,
        out_shape=(
            jax.ShapeDtypeStruct((8, 64, 512), bf16),
            jax.ShapeDtypeStruct((4, 512, 128), bf16),
            jax.ShapeDtypeStruct((2, ROWS_F, 128), bf16),
            jax.ShapeDtypeStruct((4, ROWS_S, 128), bf16),
        ),
        in_specs=[any_, pl.BlockSpec(memory_space=pltpu.SMEM), any_, any_, any_],
        out_specs=(any_,) * 4,
        scratch_shapes=[
            vmem((4, 512, 128), bf16),
            vmem((9, 768, 256), bf16),
            vmem((9, 768, 256), bf16),
            vmem((3, 512, 512), bf16),
            vmem((10, 64, 512), bf16),
            vmem((8, 64, 512), bf16),
            vmem((512, 1024), bf16),
            vmem((2, 576, 256), bf16),
            vmem((16, 192, 256), bf16),
            vmem((18, 6, 32, 768), bf16),
            vmem((1024, 256), f32),
            vmem((8, 2, 64, 256), bf16),
            vmem((2, 10, 64, 512), bf16),
            vmem((16, 4, 32, 256), bf16),
            vmem((16, 32, 256), bf16),
            vmem((256, 2048), bf16),
            vmem((18, 4, 32, 768), bf16),
            vmem((2, 3712, 128), bf16),
            vmem((4, 4, ROWS_F, 128), bf16),
            vmem((4, 2, ROWS_F, 128), bf16),
            vmem((4, ROWS_F, 128), bf16),
            vmem((2, ROWS_F, 128), bf16),
            vmem((4, ROWS_F, 128), bf16),
            vmem((4, ROWS_F, 128), bf16),
            vmem((2, ROWS_F, 128), bf16),
            vmem((4, 2, ROWS_F, 128), bf16),
            vmem((2, ROWS_F, 128), bf16),
            vmem((4, 768, 128), bf16),
            vmem((4, 768, 128), bf16),
            vmem((8, ROWS_S, 128), bf16),
            vmem((4, 4, ROWS_S, 128), bf16),
            vmem((4, ROWS_S, 128), bf16),
            vmem((4, ROWS_S, 128), bf16),
            vmem((ROWS_S, 128), bf16),
            vmem((4, ROWS_S, 128), bf16),
            vmem((8, 64, 512), bf16),
            vmem((8, 4, 64, 128), bf16),
            vmem((4, 512, 128), bf16),
            dma((4,)),
            dma((8,)), dma((8,)),
            dma((8,)), dma((8,)),
            dma((8,)), dma((8,)),
            dma, dma,
            dma, dma,
            dma, dma,
            dma, dma,
            dma((8,)), dma((8,)),
            dma((2, 8)), dma((4, 4)), dma((4, 2)),
            dma((4,)), dma((4,)), dma((2,)), dma((4,)),
            dma((2, 4)), dma((2, 4)),
            dma((2,)), dma((2,)),
            dma((3, 4)), dma((3, 4)),
            dma((2,)), dma((4,)),
            dma((4,)), dma((4,)),
            dma((8,)), dma((4,)),
            dma((4,)),
        ],
        compiler_params=pltpu.CompilerParams(
            collective_id=0, has_side_effects=True, vmem_limit_bytes=56 * 1024 * 1024
        ),
        cost_estimate=pl.CostEstimate(flops=14_000_000_000, bytes_accessed=9_000_000, transcendentals=500_000),
        name="window",
    )(
        video.reshape(4, 512, 128),
        frame_counts,
        first_weight.reshape(9, 768, 256),
        second_weight,
        cotangent.reshape(8, 64, 512),
    )
    features, grad_input, grad_first, grad_second = pl.pallas_call(
        finish,
        out_shape=(
            jax.ShapeDtypeStruct((8, 64, 512), bf16),
            jax.ShapeDtypeStruct((4, 512, 128), bf16),
            jax.ShapeDtypeStruct((432, 256), f32),
            jax.ShapeDtypeStruct((96, 512), f32),
        ),
        name="finish",
    )(features, grad_input, first, second)
    return (
        features.reshape(1, 8, 2, 32, 512),
        grad_input.reshape(1, 4, 16, 32, 128),
        grad_first,
        grad_second,
    )


def solution(mesh):
    placed = (
        P("rep", "tm", None, None, None),
        P("rep"),
        P(),
        P(),
        P("rep", None, "tm", None, None),
    )
    return jax.shard_map(
        body,
        mesh=mesh,
        in_specs=placed,
        out_specs=(
            P("rep", None, "tm", None, None),
            P("rep", "tm", None, None, None),
            P("rep", None),
            P("rep", None),
        ),
        check_vma=False,
    )
```

```python
import functools
import math

import jax
import jax.numpy as jnp
from jax import lax
from jax.experimental import pallas as pl
from jax.experimental.pallas import tpu as pltpu
from jax.sharding import PartitionSpec as P

root_half = 0.7071067811865476
MESH = pl.DeviceIdType.MESH
bf16 = jnp.bfloat16
f32 = jnp.float32

NY, NZ, NX = 4, 4, 4
ROWS_F, ROWS_S = 432, 96


def dot(a, b):
    return jnp.dot(a, b, preferred_element_type=f32)


def dot_nt(a, b):
    return lax.dot_general(a, b, (((1,), (1,)), ((), ())), preferred_element_type=f32)


def repeat(count, step):
    def run(i, carry):
        step(i)
        return carry

    lax.fori_loop(0, count, run, 0)


def put_shifted(dst, frame, rows, value, flip):
    lanes = (512, 0) if flip else (0, 512)
    wide = value.astype(f32)
    column = lax.broadcasted_iota(jnp.int32, wide.shape, 1)
    before = jnp.where(column == 0, 0.0, pltpu.roll(wide, 1, 1)).astype(bf16)
    after = jnp.where(column == 31, 0.0, pltpu.roll(wide, 31, 1)).astype(bf16)
    dst[frame, rows, :, lanes[0] : lanes[0] + 256] = before
    dst[frame, rows, :, 256:512] = value
    dst[frame, rows, :, lanes[1] : lanes[1] + 256] = after


def kernel(
    video, counts, first_w, second_w, cotangent,
    feat_out, input_out, first_sums, second_sums,
    vid, w1, w1t, w2, ctp, cts, ct_t, hown, win, xs, acc, gh, sh,
    gpc, gph, gp_t, gpx, pf, r1a, r1b, s1a, s1b, r2a, r2b, s2, r3, ag,
    px, q1, t1, q2, t2, q3, t3, ags, fout, gsend, gout,
    load_sem, win_s, win_r, ed_s, ed_r, fw_s, fw_r, cts_s, cts_r, sh_s, sh_r,
    gp_s, gp_r, gph_s, gph_r, gi_s, gi_r, f1_s, f1a_r, f1b_r, p2a_s, p2a_r, p2b_s, p2b_r,
    p3_s, p3_r, p4_s, p4_r, q1_s, q1_r, q2_s, q2_r, q3_s, q3_r, q4_s, q4_r, out_sem,
):
    rep = lax.axis_index("rep")
    tm = lax.axis_index("tm")
    y, z = rep // NZ, rep % NZ
    x, c = tm // 2, tm % 2

    def remote(src, dst, send, recv, to):
        return pltpu.make_async_remote_copy(
            src_ref=src, dst_ref=dst, send_sem=send, recv_sem=recv, device_id=to, device_id_type=MESH
        )

    def device(to_x, to_y, to_z, to_c):
        return (to_y * NZ + to_z, to_x * 2 + to_c)

    sibling = (rep, x * 2 + 1 - c)

    loads = [
        pltpu.make_async_copy(video, vid, load_sem.at[0]),
        pltpu.make_async_copy(cotangent, ctp.at[pl.ds(0, 8)], load_sem.at[1]),
        pltpu.make_async_copy(second_w, w2, load_sem.at[2]),
        pltpu.make_async_copy(first_w, w1, load_sem.at[3]),
    ]
    barrier = pltpu.get_barrier_semaphore()

    def greet(to):
        pl.semaphore_signal(barrier, inc=1, device_id=to, device_id_type=MESH)

    repeat(7, lambda i: greet((rep, (tm + 1 + i) % 8)))
    repeat(3, lambda i: greet(device(x, (y + 1 + i) % NY, z, c)))
    repeat(3, lambda i: greet(device(x, y, (z + 1 + i) % NZ, c)))

    for load in loads:
        load.start()

    live = counts[0]
    loads[0].wait()

    def keep(frame):
        return jnp.where(tm * 4 + frame < live, 1.0, 0.0).astype(f32)

    for t in range(2):
        even, odd = keep(2 * t), keep(2 * t + 1)
        hown[t, 0:32] = jnp.zeros((32, 256), bf16)
        hown[t, 544:576] = jnp.zeros((32, 256), bf16)

        def pair(n, carry):
            at = pl.ds(pl.multiple_of(n * 64, 64), 64)
            to = pl.ds(pl.multiple_of(n * 64 + 32, 32), 64)
            one = vid[2 * t, at].astype(f32) * even
            two = vid[2 * t + 1, at].astype(f32) * odd
            hown[t, to, 0:128] = ((one + two) * root_half).astype(bf16)
            hown[t, to, 128:256] = ((one - two) * root_half).astype(bf16)
            return carry

        lax.fori_loop(0, 8, pair, 0)

    pl.semaphore_wait(barrier, 13)

    def window_rows(core):
        return pl.ds(pl.multiple_of(96 * core, 32), 96)

    def frames_of(source):
        return pl.ds(2 * source, 2)

    def in_turn(i):
        step = i // 2
        return (x + step + step // 2 - 2 * (step // 3)) % 4 * 2 + (c + i) % 2

    def spread(i):
        to = in_turn((i + 1) % 8)
        rows = pl.ds(pl.multiple_of(32 * (4 * (to // 2) + 3 * (to % 2)), 32), 96)
        return remote(
            hown.at[:, rows],
            win.at[frames_of(tm), window_rows(to % 2)],
            win_s.at[to],
            win_r.at[tm],
            (rep, to),
        )

    repeat(7, lambda i: spread((i + 1) % 7).start())
    win[frames_of(tm), window_rows(c)] = hown[
        :, pl.ds(pl.multiple_of(32 * (4 * x + 3 * c), 32), 96)
    ]

    def edge_rows(core):
        return pl.ds(pl.multiple_of(64 + 32 * core, 32), 32)

    def rest_rows(core):
        return pl.ds(pl.multiple_of(128 * core, 32), 64)

    def hand_edge(source):
        block = win.at[frames_of(source), edge_rows(c)]
        return remote(block, block, ed_s.at[source], ed_r.at[source], sibling)

    def hand_rest(source):
        block = win.at[frames_of(source), rest_rows(c)]
        return remote(block, block, fw_s.at[source], fw_r.at[source], sibling)

    loads[1].wait()
    give_ct = remote(ctp.at[pl.ds(0, 8)], cts, cts_s, cts_r, sibling)
    give_ct.start()

    ctp[8:10] = jnp.zeros((2, 64, 512), bf16)
    loads[2].wait()

    def back_step(n, carry):
        grad = jnp.zeros((256, 512), f32)
        for a in range(3):
            grad = grad + dot_nt(ctp[pl.ds(4 * n + 2 - a, 4)].reshape(256, 512), w2[a])
        low, high = grad[:, :256], grad[:, 256:]
        gh[pl.ds(4 * n, 4), 0] = ((low + high) * root_half).astype(bf16).reshape(4, 64, 256)
        gh[pl.ds(4 * n, 4), 1] = ((low - high) * root_half).astype(bf16).reshape(4, 64, 256)
        return carry

    lax.fori_loop(0, 2, back_step, 0)

    loads[3].wait()

    def turn_tap(n, carry):
        for d in range(3):
            w1t[n, 256 * d : 256 * d + 256] = w1[n, 256 * d : 256 * d + 256].T
        return carry

    lax.fori_loop(0, 9, turn_tap, 0)
    ct_t[:, 0:512] = ctp[0:8].reshape(512, 512).T
    xs[0:2] = jnp.zeros((2, 6, 32, 768), bf16)
    gpx[16:18] = jnp.zeros((2, 4, 32, 768), bf16)
    for j in range(2):
        sh[j, 0:2] = jnp.zeros((2, 64, 512), bf16)
    acc[...] = jnp.zeros_like(acc)

    def take(source, row, count):
        for t in range(2):
            frame = 2 * source + t
            block = win[frame, pl.ds(pl.multiple_of(32 * row, 32), 32 * count)]
            put_shifted(xs, 2 + frame, pl.ds(row, count), block.reshape(count, 32, 256), False)

    def from_afar(i):
        source = in_turn(i)

        @pl.when(source != tm)
        def _():
            block = win.at[frames_of(source), window_rows(c)]
            remote(block, block, win_r.at[source], win_r.at[source], sibling).wait_recv()

        hand_edge(source).start()
        take(source, 3 * c, 3)

    def from_sibling(i):
        source = in_turn(i)
        hand_rest(source).start()
        block = win.at[frames_of(source), edge_rows(1 - c)]
        remote(block, block, ed_r.at[source], ed_r.at[source], sibling).wait_recv()
        take(source, 3 - c, 1)

    repeat(8, from_afar)
    repeat(8, from_sibling)

    def taps(n, carry):
        a, b = n // 3, n % 3
        acc[...] += dot(xs[pl.ds(a, 16), pl.ds(2 * c + b, 2)].reshape(1024, 768), w1[n])
        return carry

    lax.fori_loop(0, 9, taps, 0, unroll=9)

    def activate(n, carry):
        hidden = []
        for t in range(2):
            value = acc[pl.ds(pl.multiple_of(n * 128 + 64 * t, 64), 64)]
            gate = jax.nn.sigmoid(value)
            hidden.append((value * gate).astype(bf16).astype(f32))
            grad = gh[n, t].astype(f32) * (gate * (1.0 + value * (1.0 - gate)))
            gpc[2 * n + t, pl.ds(2 * c, 2)] = grad.astype(bf16).reshape(2, 32, 256)
        sh[0, 2 + n, :, 0:256] = ((hidden[0] + hidden[1]) * root_half).astype(bf16)
        sh[0, 2 + n, :, 256:512] = ((hidden[0] - hidden[1]) * root_half).astype(bf16)
        return carry

    lax.fori_loop(0, 8, activate, 0)
    own_rows = gpc.at[:, pl.ds(2 * c, 2)]
    give_gp = remote(own_rows, own_rows, gp_s, gp_r, sibling)
    give_gp.start()
    give_sh = remote(sh.at[0, pl.ds(2, 8)], sh.at[1, pl.ds(2, 8)], sh_s, sh_r, sibling)
    give_sh.start()
    give_gph = remote(gpc.at[:, 3 * c], gph, gph_s, gph_r, (rep, (tm + 7 + 2 * c) % 8))
    give_gph.start()

    def turn_rows(core):
        at = pl.ds(pl.multiple_of(core * 1024, 1024), 1024)
        gp_t[:, at] = gpc[:, pl.ds(2 * core, 2)].reshape(1024, 256).T

    turn_rows(c)

    def forward(n):
        value = jnp.zeros((256, 512), f32)
        for a in range(3):
            value = value + dot(sh[0, pl.ds(4 * n + a, 4)].reshape(256, 512), w2[a])
        fout[pl.ds(4 * n, 4)] = value.astype(bf16).reshape(4, 64, 512)

    repeat(2, forward)
    write_feat = pltpu.make_async_copy(fout, feat_out, out_sem.at[0])
    write_feat.start()

    def deliver(source, shard):
        to_y, to_z = 2 * c + shard // 4, shard % 4
        stops = (
            (0, r1a.at[y, to_z], device(x, to_y, z, c), f1a_r.at[y, to_z], to_y == y),
            (1, r1b.at[z, shard // 4], device(x, y, to_z, c), f1b_r.at[z, shard // 4], to_z == z),
        )
        for half, slot, to, sem, here in stops:

            @pl.when(here)
            def _(half=half, slot=slot, sem=sem):
                pltpu.make_async_copy(source(half, shard), slot, sem).start()

            @pl.when(jnp.logical_not(here))
            def _(half=half, slot=slot, sem=sem, to=to):
                remote(source(half, shard), slot, f1_s.at[half, shard], sem, to).start()

    def delivered(source, shard):
        to_y, to_z = 2 * c + shard // 4, shard % 4
        for half, here in ((0, to_y == y), (1, to_z == z)):

            @pl.when(jnp.logical_not(here))
            def _(half=half):
                remote(
                    source(half, shard), r1a.at[0, 0], f1_s.at[half, shard], f1_s.at[half, shard], sibling
                ).wait_send()

    def source_f(half, shard):
        return pf.at[half, pl.ds(pl.multiple_of(128 + ROWS_F * shard, 16), ROWS_F)]

    def rest_from_sibling(source):
        block = win.at[frames_of(source), rest_rows(1 - c)]
        remote(block, block, fw_r.at[source], fw_r.at[source], sibling).wait_recv()
        take(source, 4 - 4 * c, 2)

    repeat(8, rest_from_sibling)

    give_gp.wait_recv()
    turn_rows(1 - c)

    def tap(j):
        k = 13 * c + j
        a, b, d = k // 9, (k // 3) % 3, k % 3
        lanes = pl.ds(pl.multiple_of(d * 256, 256), 256)
        upper = xs[pl.ds(a, 16), pl.ds(b, 2), :, lanes].reshape(1024, 256)
        lower = xs[pl.ds(a, 16), pl.ds(b + 2, 2), :, lanes].reshape(1024, 256)
        turned = (dot(gp_t[:, 0:1024], upper) + dot(gp_t[:, 1024:2048], lower)).T.astype(bf16)
        at = pl.ds(pl.multiple_of(256 * j + 128 - 128 * c, 128), 256)
        pf[0, at] = turned[:, :128]
        pf[1, at] = turned[:, 128:]

    odd_row = y % 2

    def in_order(index, last):
        return last * odd_row + (1 - 2 * odd_row) * index

    def send_pair(pair):
        repeat(2, lambda k: deliver(source_f, in_order(2 * pair + (z + k) % 2, 7)))


    def stop_x(n, k):
        to = (x + k) % 4
        at = pl.ds(pl.multiple_of(256 * n, 256), 256)
        return remote(px.at[to, at], q1.at[x, at], q1_s.at[n, to], q1_r.at[n, x], (rep, 2 * to + c))

    def second_rows(n):
        m = 3 * c + n
        a, band = m // 2, m % 2
        lanes = pl.ds(pl.multiple_of(band * 256, 256), 256)
        own = sh[0, pl.ds(a, 8), :, lanes].reshape(512, 256)
        other = sh[1, pl.ds(a, 8), :, lanes].reshape(512, 256)
        turned = (dot(ct_t[:, 0:512], own) + dot(ct_t[:, 512:1024], other)).T.astype(bf16)
        at = pl.ds(pl.multiple_of(256 * n, 256), 256)
        for to_x in range(4):
            px[to_x, at] = turned[:, 128 * to_x : 128 * to_x + 128]
        repeat(3, lambda k: stop_x(n, k + 1).start())

    def second_taps():
        give_ct.wait_recv()
        ct_t[:, 512:1024] = cts[...].reshape(512, 512).T
        give_sh.wait_recv()
        repeat(3, second_rows)

    def first_taps(n):
        for i in range(4):
            tap(in_order(4 * n + i, 13))
        send_pair(n)

        @pl.when(n == 0)
        def _():
            second_taps()

    repeat(2, first_taps)
    q1[x] = px[x]

    def last_taps(n):
        for i in range(3):
            tap(in_order(8 + 3 * n + i, 13))
        send_pair(2 + n)

    repeat(2, last_taps)

    give_gph.wait_recv()
    inner = jnp.where((c == 0) & (x == 0) | (c == 1) & (x == 3), 0.0, 1.0).astype(bf16)

    def widen(frame, carry):
        put_shifted(gpx, frame, pl.ds(1 - c, 3), gpc[frame, pl.ds(c, 3)], True)
        put_shifted(gpx, frame, pl.ds(3 * c, 1), gph[pl.ds(frame, 1)] * inner, True)
        return carry

    lax.fori_loop(0, 16, widen, 0)
    acc[...] = jnp.zeros_like(acc)

    def input_taps(n, carry):
        a, b = n // 3, n % 3
        acc[...] += dot(gpx[pl.ds(2 - a, 16), pl.ds(2 - b, 2)].reshape(1024, 768), w1t[n])
        return carry

    lax.fori_loop(0, 9, input_taps, 0, unroll=3)

    def unpair(n, carry):
        for t in range(2):
            at = pl.ds(pl.multiple_of(n * 128 + 64 * t, 64), 64)
            low, high = acc[at, 0:128], acc[at, 128:256]
            even = jnp.where(4 * n + 2 * t < live, 1.0, 0.0).astype(f32)
            odd = jnp.where(4 * n + 2 * t + 1 < live, 1.0, 0.0).astype(f32)
            gsend[n, 2 * t] = ((low + high) * root_half * even).astype(bf16)
            gsend[n, 2 * t + 1] = ((low - high) * root_half * odd).astype(bf16)
        return carry

    lax.fori_loop(0, 8, unpair, 0)

    def pixel_rows(source):
        return gout.at[:, pl.ds(pl.multiple_of(64 * source, 64), 64)]

    def give_back(i):
        to = in_turn(i + 1)
        return remote(gsend.at[to], pixel_rows(tm), gi_s.at[to], gi_r.at[tm], (rep, to))

    repeat(7, lambda i: give_back(6 - i).start())
    gout[:, pl.ds(pl.multiple_of(64 * tm, 64), 64)] = gsend[tm]

    owner = c == y // 2

    def peer_of(i, home):
        return (home + 1 + i) % 4

    def wait_for(slot, sem):
        remote(slot, slot, sem, sem, sibling).wait_recv()

    def from_x(i):
        n, peer = i // 3, peer_of(i % 3, x)
        wait_for(q1.at[peer, pl.ds(pl.multiple_of(256 * n, 256), 256)], q1_r.at[n, peer])

    repeat(9, from_x)

    def four(ref, *index):
        total = ref[(0,) + index].astype(f32)
        for source in range(1, 4):
            total = total + ref[(source,) + index].astype(f32)
        return total.astype(bf16)

    def sum_x(i, carry):
        t1[i] = four(q1, pl.ds(pl.multiple_of(96 * i, 16), 96))
        return carry

    lax.fori_loop(0, 8, sum_x, 0)

    def give_y(i):
        return remote(
            t1.at[pl.ds(4 * i, 4)], q2.at[y], q2_s.at[i], q2_r.at[y], device(x, 2 * c + i, z, c)
        )

    def start_y(i):
        @pl.when(2 * c + i != y)
        def _():
            give_y(i).start()

        @pl.when(2 * c + i == y)
        def _():
            q2[y] = t1[pl.ds(4 * i, 4)]

    repeat(2, start_y)

    def landed(slot, sem):
        pltpu.make_async_copy(slot, slot, sem).wait()

    def give_b(i):
        return remote(s1b.at[i], r2b.at[y], p2b_s.at[i], p2b_r.at[y], device(x, 2 * c + i, z, c))

    def give_a(k):
        return remote(s1a.at[k], r2a.at[z], p2a_s.at[k], p2a_r.at[z], device(x, y, k, c))

    def give_z(k):
        return remote(t2.at[k], q3.at[z], q3_s.at[k], q3_r.at[z], device(x, y, k, c))

    def sum_b(i):
        repeat(4, lambda source: landed(r1b.at[source, i], f1b_r.at[source, i]))
        s1b[i] = four(r1b, i)

        @pl.when(2 * c + i != y)
        def _():
            give_b(i).start()

        @pl.when(2 * c + i == y)
        def _():
            r2b[y] = s1b[i]

    sum_b(odd_row)

    @pl.when(owner)
    def _():
        def sum_a(k):
            repeat(4, lambda source: landed(r1a.at[source, k], f1a_r.at[source, k]))
            s1a[k] = four(r1a, k)

            @pl.when(k != z)
            def _():
                give_a(k).start()

        repeat(4, lambda k: sum_a((z + 1 + k) % 4))
        r2a[z] = s1a[z]

    sum_b(1 - odd_row)

    @pl.when(owner)
    def _():
        repeat(3, lambda i: wait_for(q2.at[peer_of(i, y)], q2_r.at[peer_of(i, y)]))

        def sum_y(k):
            t2[k] = four(q2, k)

            @pl.when(k != z)
            def _():
                give_z(k).start()

        repeat(4, lambda k: sum_y((z + 1 + k) % 4))
        q3[z] = t2[z]

    def give_x(half, k):
        slot = r3.at[x, half]
        return remote(s2.at[half], slot, p3_s.at[half, k], p3_r.at[half, x], (rep, (x + k) % 4 * 2 + c))

    def give_second(k):
        return remote(t3, ags.at[x], q4_s.at[k], q4_r.at[x], (rep, (tm + k) % 8))

    def give_first(half):
        return remote(ag.at[half], ag.at[half], p4_s.at[half], p4_r.at[half], sibling)

    @pl.when(owner)
    def _():
        for half, slots, sems, home in ((0, r2a, p2a_r, z), (1, r2b, p2b_r, y)):
            repeat(3, lambda i: wait_for(slots.at[peer_of(i, home)], sems.at[peer_of(i, home)]))
            s2[half] = four(slots)
            repeat(3, lambda i: give_x(half, (i + 1) % 3 + 1).start())
        r3[x] = s2[...]
        repeat(3, lambda i: wait_for(q3.at[peer_of(i, z)], q3_r.at[peer_of(i, z)]))
        t3[...] = four(q3)
        repeat(7, lambda i: give_second(i + 1).start())
        ags[x] = t3[...]

    def from_rows(i):
        source = in_turn((tm + 1 + i) % 8)

        @pl.when(source != tm)
        def _():
            wait_for(pixel_rows(source), gi_r.at[source])

    repeat(8, from_rows)
    write_input = pltpu.make_async_copy(gout, input_out, out_sem.at[1])
    write_input.start()

    for copy in [give_ct, give_gp, give_sh, give_gph]:
        copy.wait_send()
    repeat(7, lambda i: spread(i).wait_send())
    repeat(7, lambda i: give_back(i).wait_send())
    repeat(9, lambda i: stop_x(i // 3, i % 3 + 1).wait_send())

    def drain_hand(source):
        hand_edge(source).wait_send()
        hand_rest(source).wait_send()

    repeat(8, drain_hand)
    repeat(8, lambda shard: delivered(source_f, shard))

    def drain_y(i):
        @pl.when(2 * c + i != y)
        def _():
            give_y(i).wait_send()
            give_b(i).wait_send()

    repeat(2, drain_y)

    @pl.when(owner)
    def _():
        def drain_z(i):
            k = peer_of(i, z)
            give_a(k).wait_send()
            give_z(k).wait_send()

        repeat(3, drain_z)
        def sum_half(half):
            repeat(3, lambda i: wait_for(r3.at[peer_of(i, x), half], p3_r.at[half, peer_of(i, x)]))
            ag[half] = four(r3, half)
            give_first(half).start()

        repeat(2, sum_half)

    @pl.when(jnp.logical_not(owner))
    def _():
        repeat(2, lambda half: give_first(half).wait_recv())

    write_first = pltpu.make_async_copy(ag, first_sums, out_sem.at[2])
    write_first.start()

    def take_sums(peer):
        @pl.when(jnp.logical_not(owner) | (peer != x))
        def _():
            wait_for(ags.at[peer], q4_r.at[peer])

    repeat(4, take_sums)
    write_second = pltpu.make_async_copy(ags, second_sums, out_sem.at[3])
    write_second.start()

    @pl.when(owner)
    def _():
        repeat(6, lambda i: give_x(i // 3, i % 3 + 1).wait_send())
        repeat(7, lambda i: give_second(i + 1).wait_send())
        repeat(2, lambda half: give_first(half).wait_send())

    for write in (write_feat, write_input, write_first, write_second):
        write.wait()


def finish(features, grad_input, first, second, feat_out, input_out, first_out, second_out):
    feat_out[...] = features[...]
    input_out[...] = grad_input[...]
    scale_first = 1.0 / math.sqrt(131072)
    scale_second = 1.0 / math.sqrt(65536)
    for half in range(2):
        first_out[:, 128 * half : 128 * half + 128] = first[half].astype(f32) * scale_first
    for quarter in range(4):
        second_out[:, 128 * quarter : 128 * quarter + 128] = second[quarter].astype(f32) * scale_second


def body(video, frame_counts, first_weight, second_weight, cotangent):
    any_ = pl.BlockSpec(memory_space=pl.ANY)
    vmem = pltpu.VMEM
    dma = pltpu.SemaphoreType.DMA
    features, grad_input, first, second = pl.pallas_call(
        kernel,
        out_shape=(
            jax.ShapeDtypeStruct((8, 64, 512), bf16),
            jax.ShapeDtypeStruct((4, 512, 128), bf16),
            jax.ShapeDtypeStruct((2, ROWS_F, 128), bf16),
            jax.ShapeDtypeStruct((4, ROWS_S, 128), bf16),
        ),
        in_specs=[any_, pl.BlockSpec(memory_space=pltpu.SMEM), any_, any_, any_],
        out_specs=(any_,) * 4,
        scratch_shapes=[
            vmem((4, 512, 128), bf16),
            vmem((9, 768, 256), bf16),
            vmem((9, 768, 256), bf16),
            vmem((3, 512, 512), bf16),
            vmem((10, 64, 512), bf16),
            vmem((8, 64, 512), bf16),
            vmem((512, 1024), bf16),
            vmem((2, 576, 256), bf16),
            vmem((16, 192, 256), bf16),
            vmem((18, 6, 32, 768), bf16),
            vmem((1024, 256), f32),
            vmem((8, 2, 64, 256), bf16),
            vmem((2, 10, 64, 512), bf16),
            vmem((16, 4, 32, 256), bf16),
            vmem((16, 32, 256), bf16),
            vmem((256, 2048), bf16),
            vmem((18, 4, 32, 768), bf16),
            vmem((2, 3712, 128), bf16),
            vmem((4, 4, ROWS_F, 128), bf16),
            vmem((4, 2, ROWS_F, 128), bf16),
            vmem((4, ROWS_F, 128), bf16),
            vmem((2, ROWS_F, 128), bf16),
            vmem((4, ROWS_F, 128), bf16),
            vmem((4, ROWS_F, 128), bf16),
            vmem((2, ROWS_F, 128), bf16),
            vmem((4, 2, ROWS_F, 128), bf16),
            vmem((2, ROWS_F, 128), bf16),
            vmem((4, 768, 128), bf16),
            vmem((4, 768, 128), bf16),
            vmem((8, ROWS_S, 128), bf16),
            vmem((4, 4, ROWS_S, 128), bf16),
            vmem((4, ROWS_S, 128), bf16),
            vmem((4, ROWS_S, 128), bf16),
            vmem((ROWS_S, 128), bf16),
            vmem((4, ROWS_S, 128), bf16),
            vmem((8, 64, 512), bf16),
            vmem((8, 4, 64, 128), bf16),
            vmem((4, 512, 128), bf16),
            dma((4,)),
            dma((8,)), dma((8,)),
            dma((8,)), dma((8,)),
            dma((8,)), dma((8,)),
            dma, dma,
            dma, dma,
            dma, dma,
            dma, dma,
            dma((8,)), dma((8,)),
            dma((2, 8)), dma((4, 4)), dma((4, 2)),
            dma((4,)), dma((4,)), dma((2,)), dma((4,)),
            dma((2, 4)), dma((2, 4)),
            dma((2,)), dma((2,)),
            dma((3, 4)), dma((3, 4)),
            dma((2,)), dma((4,)),
            dma((4,)), dma((4,)),
            dma((8,)), dma((4,)),
            dma((4,)),
        ],
        compiler_params=pltpu.CompilerParams(
            collective_id=0, has_side_effects=True, vmem_limit_bytes=56 * 1024 * 1024
        ),
        cost_estimate=pl.CostEstimate(flops=14_000_000_000, bytes_accessed=9_000_000, transcendentals=500_000),
        name="window",
    )(
        video.reshape(4, 512, 128),
        frame_counts,
        first_weight.reshape(9, 768, 256),
        second_weight,
        cotangent.reshape(8, 64, 512),
    )
    features, grad_input, grad_first, grad_second = pl.pallas_call(
        finish,
        out_shape=(
            jax.ShapeDtypeStruct((8, 64, 512), bf16),
            jax.ShapeDtypeStruct((4, 512, 128), bf16),
            jax.ShapeDtypeStruct((432, 256), f32),
            jax.ShapeDtypeStruct((96, 512), f32),
        ),
        name="finish",
    )(features, grad_input, first, second)
    return (
        features.reshape(1, 8, 2, 32, 512),
        grad_input.reshape(1, 4, 16, 32, 128),
        grad_first,
        grad_second,
    )


def solution(mesh):
    placed = (
        P("rep", "tm", None, None, None),
        P("rep"),
        P(),
        P(),
        P("rep", None, "tm", None, None),
    )
    return jax.shard_map(
        body,
        mesh=mesh,
        in_specs=placed,
        out_specs=(
            P("rep", None, "tm", None, None),
            P("rep", "tm", None, None, None),
            P("rep", None),
            P("rep", None),
        ),
        check_vma=False,
    )
```

```python
import functools
import math

import jax
import jax.numpy as jnp
from jax import lax
from jax.experimental import pallas as pl
from jax.experimental.pallas import tpu as pltpu
from jax.sharding import PartitionSpec as P

root_half = 0.7071067811865476
MESH = pl.DeviceIdType.MESH
bf16 = jnp.bfloat16
f32 = jnp.float32

NY, NZ, NX = 4, 4, 4
ROWS_F, ROWS_S = 432, 96


def dot(a, b):
    return jnp.dot(a, b, preferred_element_type=f32)


def dot_nt(a, b):
    return lax.dot_general(a, b, (((1,), (1,)), ((), ())), preferred_element_type=f32)


def repeat(count, step):
    def run(i, carry):
        step(i)
        return carry

    lax.fori_loop(0, count, run, 0)


def put_shifted(dst, frame, rows, value, flip):
    lanes = (512, 0) if flip else (0, 512)
    wide = value.astype(f32)
    column = lax.broadcasted_iota(jnp.int32, wide.shape, 1)
    before = jnp.where(column == 0, 0.0, pltpu.roll(wide, 1, 1)).astype(bf16)
    after = jnp.where(column == 31, 0.0, pltpu.roll(wide, 31, 1)).astype(bf16)
    dst[frame, rows, :, lanes[0] : lanes[0] + 256] = before
    dst[frame, rows, :, 256:512] = value
    dst[frame, rows, :, lanes[1] : lanes[1] + 256] = after


def kernel(
    video, counts, first_w, second_w, cotangent,
    feat_out, input_out, first_sums, second_sums,
    vid, w1, w1t, w2, ctp, cts, ct_t, hown, win, xs, acc, gh, sh,
    gpc, gph, gp_t, gpx, pf, r1a, r1b, s1a, s1b, r2a, r2b, s2, r3, ag,
    px, q1, t1, q2, t2, q3, t3, ags, fout, gsend, gout,
    load_sem, win_s, win_r, ed_s, ed_r, fw_s, fw_r, cts_s, cts_r, sh_s, sh_r,
    gp_s, gp_r, gph_s, gph_r, gi_s, gi_r, f1_s, f1a_r, f1b_r, p2a_s, p2a_r, p2b_s, p2b_r,
    p3_s, p3_r, p4_s, p4_r, q1_s, q1_r, q2_s, q2_r, q3_s, q3_r, q4_s, q4_r, out_sem,
):
    rep = lax.axis_index("rep")
    tm = lax.axis_index("tm")
    y, z = rep // NZ, rep % NZ
    x, c = tm // 2, tm % 2

    def remote(src, dst, send, recv, to):
        return pltpu.make_async_remote_copy(
            src_ref=src, dst_ref=dst, send_sem=send, recv_sem=recv, device_id=to, device_id_type=MESH
        )

    def device(to_x, to_y, to_z, to_c):
        return (to_y * NZ + to_z, to_x * 2 + to_c)

    sibling = (rep, x * 2 + 1 - c)

    loads = [
        pltpu.make_async_copy(video, vid, load_sem.at[0]),
        pltpu.make_async_copy(cotangent, ctp.at[pl.ds(0, 8)], load_sem.at[1]),
        pltpu.make_async_copy(second_w, w2, load_sem.at[2]),
        pltpu.make_async_copy(first_w, w1, load_sem.at[3]),
    ]
    barrier = pltpu.get_barrier_semaphore()

    def greet(to):
        pl.semaphore_signal(barrier, inc=1, device_id=to, device_id_type=MESH)

    repeat(7, lambda i: greet((rep, (tm + 1 + i) % 8)))
    repeat(3, lambda i: greet(device(x, (y + 1 + i) % NY, z, c)))
    repeat(3, lambda i: greet(device(x, y, (z + 1 + i) % NZ, c)))

    for load in loads:
        load.start()

    live = counts[0]
    loads[0].wait()

    def keep(frame):
        return jnp.where(tm * 4 + frame < live, 1.0, 0.0).astype(f32)

    for t in range(2):
        even, odd = keep(2 * t), keep(2 * t + 1)
        hown[t, 0:32] = jnp.zeros((32, 256), bf16)
        hown[t, 544:576] = jnp.zeros((32, 256), bf16)

        def pair(n, carry):
            at = pl.ds(pl.multiple_of(n * 64, 64), 64)
            to = pl.ds(pl.multiple_of(n * 64 + 32, 32), 64)
            one = vid[2 * t, at].astype(f32) * even
            two = vid[2 * t + 1, at].astype(f32) * odd
            hown[t, to, 0:128] = ((one + two) * root_half).astype(bf16)
            hown[t, to, 128:256] = ((one - two) * root_half).astype(bf16)
            return carry

        lax.fori_loop(0, 8, pair, 0)

    pl.semaphore_wait(barrier, 13)

    def window_rows(core):
        return pl.ds(pl.multiple_of(96 * core, 32), 96)

    def frames_of(source):
        return pl.ds(2 * source, 2)

    def in_turn(i):
        step = i // 2
        return (x + step + step // 2 - 2 * (step // 3)) % 4 * 2 + (c + i) % 2

    def spread(i):
        to = in_turn((i + 1) % 8)
        rows = pl.ds(pl.multiple_of(32 * (4 * (to // 2) + 3 * (to % 2)), 32), 96)
        return remote(
            hown.at[:, rows],
            win.at[frames_of(tm), window_rows(to % 2)],
            win_s.at[to],
            win_r.at[tm],
            (rep, to),
        )

    repeat(7, lambda i: spread((i + 1) % 7).start())
    win[frames_of(tm), window_rows(c)] = hown[
        :, pl.ds(pl.multiple_of(32 * (4 * x + 3 * c), 32), 96)
    ]

    def edge_rows(core):
        return pl.ds(pl.multiple_of(64 + 32 * core, 32), 32)

    def rest_rows(core):
        return pl.ds(pl.multiple_of(128 * core, 32), 64)

    def hand_edge(source):
        block = win.at[frames_of(source), edge_rows(c)]
        return remote(block, block, ed_s.at[source], ed_r.at[source], sibling)

    def hand_rest(source):
        block = win.at[frames_of(source), rest_rows(c)]
        return remote(block, block, fw_s.at[source], fw_r.at[source], sibling)

    loads[1].wait()
    give_ct = remote(ctp.at[pl.ds(0, 8)], cts, cts_s, cts_r, sibling)
    give_ct.start()

    ctp[8:10] = jnp.zeros((2, 64, 512), bf16)
    loads[2].wait()

    def back_step(n, carry):
        grad = jnp.zeros((256, 512), f32)
        for a in range(3):
            grad = grad + dot_nt(ctp[pl.ds(4 * n + 2 - a, 4)].reshape(256, 512), w2[a])
        low, high = grad[:, :256], grad[:, 256:]
        gh[pl.ds(4 * n, 4), 0] = ((low + high) * root_half).astype(bf16).reshape(4, 64, 256)
        gh[pl.ds(4 * n, 4), 1] = ((low - high) * root_half).astype(bf16).reshape(4, 64, 256)
        return carry

    lax.fori_loop(0, 2, back_step, 0)

    loads[3].wait()

    def turn_tap(n, carry):
        for d in range(3):
            w1t[n, 256 * d : 256 * d + 256] = w1[n, 256 * d : 256 * d + 256].T
        return carry

    lax.fori_loop(0, 9, turn_tap, 0)
    ct_t[:, 0:512] = ctp[0:8].reshape(512, 512).T
    xs[0:2] = jnp.zeros((2, 6, 32, 768), bf16)
    gpx[16:18] = jnp.zeros((2, 4, 32, 768), bf16)
    for j in range(2):
        sh[j, 0:2] = jnp.zeros((2, 64, 512), bf16)
    acc[...] = jnp.zeros_like(acc)

    def take(source, row, count):
        for t in range(2):
            frame = 2 * source + t
            block = win[frame, pl.ds(pl.multiple_of(32 * row, 32), 32 * count)]
            put_shifted(xs, 2 + frame, pl.ds(row, count), block.reshape(count, 32, 256), False)

    def from_afar(i):
        source = in_turn(i)

        @pl.when(source != tm)
        def _():
            block = win.at[frames_of(source), window_rows(c)]
            remote(block, block, win_r.at[source], win_r.at[source], sibling).wait_recv()

        hand_edge(source).start()
        take(source, 3 * c, 3)

    def from_sibling(i):
        source = in_turn(i)
        hand_rest(source).start()
        block = win.at[frames_of(source), edge_rows(1 - c)]
        remote(block, block, ed_r.at[source], ed_r.at[source], sibling).wait_recv()
        take(source, 3 - c, 1)

    repeat(8, from_afar)
    repeat(8, from_sibling)

    def taps(n, carry):
        a, b = n // 3, n % 3
        acc[...] += dot(xs[pl.ds(a, 16), pl.ds(2 * c + b, 2)].reshape(1024, 768), w1[n])
        return carry

    lax.fori_loop(0, 9, taps, 0, unroll=9)

    def activate(n, carry):
        hidden = []
        for t in range(2):
            value = acc[pl.ds(pl.multiple_of(n * 128 + 64 * t, 64), 64)]
            gate = jax.nn.sigmoid(value)
            hidden.append((value * gate).astype(bf16).astype(f32))
            grad = gh[n, t].astype(f32) * (gate * (1.0 + value * (1.0 - gate)))
            gpc[2 * n + t, pl.ds(2 * c, 2)] = grad.astype(bf16).reshape(2, 32, 256)
        sh[0, 2 + n, :, 0:256] = ((hidden[0] + hidden[1]) * root_half).astype(bf16)
        sh[0, 2 + n, :, 256:512] = ((hidden[0] - hidden[1]) * root_half).astype(bf16)
        return carry

    lax.fori_loop(0, 8, activate, 0)
    own_rows = gpc.at[:, pl.ds(2 * c, 2)]
    give_gp = remote(own_rows, own_rows, gp_s, gp_r, sibling)
    give_gp.start()
    give_sh = remote(sh.at[0, pl.ds(2, 8)], sh.at[1, pl.ds(2, 8)], sh_s, sh_r, sibling)
    give_sh.start()
    give_gph = remote(gpc.at[:, 3 * c], gph, gph_s, gph_r, (rep, (tm + 7 + 2 * c) % 8))
    give_gph.start()

    def turn_rows(core):
        at = pl.ds(pl.multiple_of(core * 1024, 1024), 1024)
        gp_t[:, at] = gpc[:, pl.ds(2 * core, 2)].reshape(1024, 256).T

    turn_rows(c)

    def forward(n):
        value = jnp.zeros((256, 512), f32)
        for a in range(3):
            value = value + dot(sh[0, pl.ds(4 * n + a, 4)].reshape(256, 512), w2[a])
        fout[pl.ds(4 * n, 4)] = value.astype(bf16).reshape(4, 64, 512)

    repeat(2, forward)
    write_feat = pltpu.make_async_copy(fout, feat_out, out_sem.at[0])
    write_feat.start()

    def deliver(source, shard):
        to_y, to_z = 2 * c + shard // 4, shard % 4
        stops = (
            (0, r1a.at[y, to_z], device(x, to_y, z, c), f1a_r.at[y, to_z], to_y == y),
            (1, r1b.at[z, shard // 4], device(x, y, to_z, c), f1b_r.at[z, shard // 4], to_z == z),
        )
        for half, slot, to, sem, here in stops:

            @pl.when(here)
            def _(half=half, slot=slot, sem=sem):
                pltpu.make_async_copy(source(half, shard), slot, sem).start()

            @pl.when(jnp.logical_not(here))
            def _(half=half, slot=slot, sem=sem, to=to):
                remote(source(half, shard), slot, f1_s.at[half, shard], sem, to).start()

    def delivered(source, shard):
        to_y, to_z = 2 * c + shard // 4, shard % 4
        for half, here in ((0, to_y == y), (1, to_z == z)):

            @pl.when(jnp.logical_not(here))
            def _(half=half):
                remote(
                    source(half, shard), r1a.at[0, 0], f1_s.at[half, shard], f1_s.at[half, shard], sibling
                ).wait_send()

    def source_f(half, shard):
        return pf.at[half, pl.ds(pl.multiple_of(128 + ROWS_F * shard, 16), ROWS_F)]

    def rest_from_sibling(source):
        block = win.at[frames_of(source), rest_rows(1 - c)]
        remote(block, block, fw_r.at[source], fw_r.at[source], sibling).wait_recv()
        take(source, 4 - 4 * c, 2)

    repeat(8, rest_from_sibling)

    give_gp.wait_recv()
    turn_rows(1 - c)

    def tap(j):
        k = 13 * c + j
        a, b, d = k // 9, (k // 3) % 3, k % 3
        lanes = pl.ds(pl.multiple_of(d * 256, 256), 256)
        upper = xs[pl.ds(a, 16), pl.ds(b, 2), :, lanes].reshape(1024, 256)
        lower = xs[pl.ds(a, 16), pl.ds(b + 2, 2), :, lanes].reshape(1024, 256)
        turned = (dot(gp_t[:, 0:1024], upper) + dot(gp_t[:, 1024:2048], lower)).T.astype(bf16)
        at = pl.ds(pl.multiple_of(256 * j + 128 - 128 * c, 128), 256)
        pf[0, at] = turned[:, :128]
        pf[1, at] = turned[:, 128:]

    odd_row = y % 2

    def in_order(index, last):
        return last * odd_row + (1 - 2 * odd_row) * index

    def send_pair(pair):
        repeat(2, lambda k: deliver(source_f, in_order(2 * pair + (z + k) % 2, 7)))


    def stop_x(n, k):
        to = (x + k) % 4
        at = pl.ds(pl.multiple_of(256 * n, 256), 256)
        return remote(px.at[to, at], q1.at[x, at], q1_s.at[n, to], q1_r.at[n, x], (rep, 2 * to + c))

    def second_rows(n):
        m = 3 * c + n
        a, band = m // 2, m % 2
        lanes = pl.ds(pl.multiple_of(band * 256, 256), 256)
        own = sh[0, pl.ds(a, 8), :, lanes].reshape(512, 256)
        other = sh[1, pl.ds(a, 8), :, lanes].reshape(512, 256)
        turned = (dot(ct_t[:, 0:512], own) + dot(ct_t[:, 512:1024], other)).T.astype(bf16)
        at = pl.ds(pl.multiple_of(256 * n, 256), 256)
        for to_x in range(4):
            px[to_x, at] = turned[:, 128 * to_x : 128 * to_x + 128]
        repeat(3, lambda k: stop_x(n, (k + 1) % 3 + 1).start())

    def second_taps():
        give_ct.wait_recv()
        ct_t[:, 512:1024] = cts[...].reshape(512, 512).T
        give_sh.wait_recv()
        repeat(3, second_rows)

    def first_taps(n):
        for i in range(4):
            tap(in_order(4 * n + i, 13))
        send_pair(n)

        @pl.when(n == 0)
        def _():
            second_taps()

    repeat(2, first_taps)
    q1[x] = px[x]

    def last_taps(n):
        for i in range(3):
            tap(in_order(8 + 3 * n + i, 13))
        send_pair(2 + n)

    repeat(2, last_taps)

    give_gph.wait_recv()
    inner = jnp.where((c == 0) & (x == 0) | (c == 1) & (x == 3), 0.0, 1.0).astype(bf16)

    def widen(frame, carry):
        put_shifted(gpx, frame, pl.ds(1 - c, 3), gpc[frame, pl.ds(c, 3)], True)
        put_shifted(gpx, frame, pl.ds(3 * c, 1), gph[pl.ds(frame, 1)] * inner, True)
        return carry

    lax.fori_loop(0, 16, widen, 0)
    acc[...] = jnp.zeros_like(acc)

    def input_taps(n, carry):
        a, b = n // 3, n % 3
        acc[...] += dot(gpx[pl.ds(2 - a, 16), pl.ds(2 - b, 2)].reshape(1024, 768), w1t[n])
        return carry

    lax.fori_loop(0, 9, input_taps, 0, unroll=3)

    def unpair(n, carry):
        for t in range(2):
            at = pl.ds(pl.multiple_of(n * 128 + 64 * t, 64), 64)
            low, high = acc[at, 0:128], acc[at, 128:256]
            even = jnp.where(4 * n + 2 * t < live, 1.0, 0.0).astype(f32)
            odd = jnp.where(4 * n + 2 * t + 1 < live, 1.0, 0.0).astype(f32)
            gsend[n, 2 * t] = ((low + high) * root_half * even).astype(bf16)
            gsend[n, 2 * t + 1] = ((low - high) * root_half * odd).astype(bf16)
        return carry

    lax.fori_loop(0, 8, unpair, 0)

    def pixel_rows(source):
        return gout.at[:, pl.ds(pl.multiple_of(64 * source, 64), 64)]

    def give_back(i):
        to = in_turn(i + 1)
        return remote(gsend.at[to], pixel_rows(tm), gi_s.at[to], gi_r.at[tm], (rep, to))

    repeat(7, lambda i: give_back(6 - i).start())
    gout[:, pl.ds(pl.multiple_of(64 * tm, 64), 64)] = gsend[tm]

    owner = c == y // 2

    def peer_of(i, home):
        return (home + 1 + i) % 4

    def wait_for(slot, sem):
        remote(slot, slot, sem, sem, sibling).wait_recv()

    def from_x(i):
        n, peer = i // 3, peer_of(i % 3, x)
        wait_for(q1.at[peer, pl.ds(pl.multiple_of(256 * n, 256), 256)], q1_r.at[n, peer])


    def four(ref, *index):
        total = ref[(0,) + index].astype(f32)
        for source in range(1, 4):
            total = total + ref[(source,) + index].astype(f32)
        return total.astype(bf16)

    def sum_x(i, carry):
        t1[i] = four(q1, pl.ds(pl.multiple_of(96 * i, 16), 96))
        return carry


    def give_y(i):
        return remote(
            t1.at[pl.ds(4 * i, 4)], q2.at[y], q2_s.at[i], q2_r.at[y], device(x, 2 * c + i, z, c)
        )

    def start_y(i):
        @pl.when(2 * c + i != y)
        def _():
            give_y(i).start()

        @pl.when(2 * c + i == y)
        def _():
            q2[y] = t1[pl.ds(4 * i, 4)]


    def landed(slot, sem):
        pltpu.make_async_copy(slot, slot, sem).wait()

    def give_b(i):
        return remote(s1b.at[i], r2b.at[y], p2b_s.at[i], p2b_r.at[y], device(x, 2 * c + i, z, c))

    def give_a(k):
        return remote(s1a.at[k], r2a.at[z], p2a_s.at[k], p2a_r.at[z], device(x, y, k, c))

    def give_z(k):
        return remote(t2.at[k], q3.at[z], q3_s.at[k], q3_r.at[z], device(x, y, k, c))

    def sum_b(i):
        repeat(4, lambda source: landed(r1b.at[source, i], f1b_r.at[source, i]))
        s1b[i] = four(r1b, i)

        @pl.when(2 * c + i != y)
        def _():
            give_b(i).start()

        @pl.when(2 * c + i == y)
        def _():
            r2b[y] = s1b[i]

    sum_b(odd_row)
    repeat(9, from_x)
    lax.fori_loop(0, 8, sum_x, 0)
    repeat(2, start_y)

    @pl.when(owner)
    def _():
        def sum_a(k):
            repeat(4, lambda source: landed(r1a.at[source, k], f1a_r.at[source, k]))
            s1a[k] = four(r1a, k)

            @pl.when(k != z)
            def _():
                give_a(k).start()

        repeat(4, lambda k: sum_a((z + 1 + k) % 4))
        r2a[z] = s1a[z]

    sum_b(1 - odd_row)

    @pl.when(owner)
    def _():
        repeat(3, lambda i: wait_for(q2.at[peer_of(i, y)], q2_r.at[peer_of(i, y)]))

        def sum_y(k):
            t2[k] = four(q2, k)

            @pl.when(k != z)
            def _():
                give_z(k).start()

        repeat(4, lambda k: sum_y((z + 1 + k) % 4))
        q3[z] = t2[z]

    def give_x(half, k):
        slot = r3.at[x, half]
        return remote(s2.at[half], slot, p3_s.at[half, k], p3_r.at[half, x], (rep, (x + k) % 4 * 2 + c))

    def give_second(k):
        return remote(t3, ags.at[x], q4_s.at[k], q4_r.at[x], (rep, (tm + k) % 8))

    def give_first(half):
        return remote(ag.at[half], ag.at[half], p4_s.at[half], p4_r.at[half], sibling)

    @pl.when(owner)
    def _():
        for half, slots, sems, home in ((0, r2a, p2a_r, z), (1, r2b, p2b_r, y)):
            repeat(3, lambda i: wait_for(slots.at[peer_of(i, home)], sems.at[peer_of(i, home)]))
            s2[half] = four(slots)
            repeat(3, lambda i: give_x(half, (i + 1) % 3 + 1).start())
        r3[x] = s2[...]
        repeat(3, lambda i: wait_for(q3.at[peer_of(i, z)], q3_r.at[peer_of(i, z)]))
        t3[...] = four(q3)
        repeat(7, lambda i: give_second(i + 1).start())
        ags[x] = t3[...]

    def from_rows(i):
        source = in_turn((tm + 1 + i) % 8)

        @pl.when(source != tm)
        def _():
            wait_for(pixel_rows(source), gi_r.at[source])

    repeat(8, from_rows)
    write_input = pltpu.make_async_copy(gout, input_out, out_sem.at[1])
    write_input.start()

    for copy in [give_ct, give_gp, give_sh, give_gph]:
        copy.wait_send()
    repeat(7, lambda i: spread(i).wait_send())
    repeat(7, lambda i: give_back(i).wait_send())
    repeat(9, lambda i: stop_x(i // 3, i % 3 + 1).wait_send())

    def drain_hand(source):
        hand_edge(source).wait_send()
        hand_rest(source).wait_send()

    repeat(8, drain_hand)
    repeat(8, lambda shard: delivered(source_f, shard))

    def drain_y(i):
        @pl.when(2 * c + i != y)
        def _():
            give_y(i).wait_send()
            give_b(i).wait_send()

    repeat(2, drain_y)

    @pl.when(owner)
    def _():
        def drain_z(i):
            k = peer_of(i, z)
            give_a(k).wait_send()
            give_z(k).wait_send()

        repeat(3, drain_z)
        def sum_half(half):
            repeat(3, lambda i: wait_for(r3.at[peer_of(i, x), half], p3_r.at[half, peer_of(i, x)]))
            ag[half] = four(r3, half)
            give_first(half).start()

        repeat(2, sum_half)

    @pl.when(jnp.logical_not(owner))
    def _():
        repeat(2, lambda half: give_first(half).wait_recv())

    write_first = pltpu.make_async_copy(ag, first_sums, out_sem.at[2])
    write_first.start()

    def take_sums(peer):
        @pl.when(jnp.logical_not(owner) | (peer != x))
        def _():
            wait_for(ags.at[peer], q4_r.at[peer])

    repeat(4, take_sums)
    write_second = pltpu.make_async_copy(ags, second_sums, out_sem.at[3])
    write_second.start()

    @pl.when(owner)
    def _():
        repeat(6, lambda i: give_x(i // 3, i % 3 + 1).wait_send())
        repeat(7, lambda i: give_second(i + 1).wait_send())
        repeat(2, lambda half: give_first(half).wait_send())

    for write in (write_feat, write_input, write_first, write_second):
        write.wait()


def finish(features, grad_input, first, second, feat_out, input_out, first_out, second_out):
    feat_out[...] = features[...]
    input_out[...] = grad_input[...]
    scale_first = 1.0 / math.sqrt(131072)
    scale_second = 1.0 / math.sqrt(65536)
    for half in range(2):
        first_out[:, 128 * half : 128 * half + 128] = first[half].astype(f32) * scale_first
    for quarter in range(4):
        second_out[:, 128 * quarter : 128 * quarter + 128] = second[quarter].astype(f32) * scale_second


def body(video, frame_counts, first_weight, second_weight, cotangent):
    any_ = pl.BlockSpec(memory_space=pl.ANY)
    vmem = pltpu.VMEM
    dma = pltpu.SemaphoreType.DMA
    features, grad_input, first, second = pl.pallas_call(
        kernel,
        out_shape=(
            jax.ShapeDtypeStruct((8, 64, 512), bf16),
            jax.ShapeDtypeStruct((4, 512, 128), bf16),
            jax.ShapeDtypeStruct((2, ROWS_F, 128), bf16),
            jax.ShapeDtypeStruct((4, ROWS_S, 128), bf16),
        ),
        in_specs=[any_, pl.BlockSpec(memory_space=pltpu.SMEM), any_, any_, any_],
        out_specs=(any_,) * 4,
        scratch_shapes=[
            vmem((4, 512, 128), bf16),
            vmem((9, 768, 256), bf16),
            vmem((9, 768, 256), bf16),
            vmem((3, 512, 512), bf16),
            vmem((10, 64, 512), bf16),
            vmem((8, 64, 512), bf16),
            vmem((512, 1024), bf16),
            vmem((2, 576, 256), bf16),
            vmem((16, 192, 256), bf16),
            vmem((18, 6, 32, 768), bf16),
            vmem((1024, 256), f32),
            vmem((8, 2, 64, 256), bf16),
            vmem((2, 10, 64, 512), bf16),
            vmem((16, 4, 32, 256), bf16),
            vmem((16, 32, 256), bf16),
            vmem((256, 2048), bf16),
            vmem((18, 4, 32, 768), bf16),
            vmem((2, 3712, 128), bf16),
            vmem((4, 4, ROWS_F, 128), bf16),
            vmem((4, 2, ROWS_F, 128), bf16),
            vmem((4, ROWS_F, 128), bf16),
            vmem((2, ROWS_F, 128), bf16),
            vmem((4, ROWS_F, 128), bf16),
            vmem((4, ROWS_F, 128), bf16),
            vmem((2, ROWS_F, 128), bf16),
            vmem((4, 2, ROWS_F, 128), bf16),
            vmem((2, ROWS_F, 128), bf16),
            vmem((4, 768, 128), bf16),
            vmem((4, 768, 128), bf16),
            vmem((8, ROWS_S, 128), bf16),
            vmem((4, 4, ROWS_S, 128), bf16),
            vmem((4, ROWS_S, 128), bf16),
            vmem((4, ROWS_S, 128), bf16),
            vmem((ROWS_S, 128), bf16),
            vmem((4, ROWS_S, 128), bf16),
            vmem((8, 64, 512), bf16),
            vmem((8, 4, 64, 128), bf16),
            vmem((4, 512, 128), bf16),
            dma((4,)),
            dma((8,)), dma((8,)),
            dma((8,)), dma((8,)),
            dma((8,)), dma((8,)),
            dma, dma,
            dma, dma,
            dma, dma,
            dma, dma,
            dma((8,)), dma((8,)),
            dma((2, 8)), dma((4, 4)), dma((4, 2)),
            dma((4,)), dma((4,)), dma((2,)), dma((4,)),
            dma((2, 4)), dma((2, 4)),
            dma((2,)), dma((2,)),
            dma((3, 4)), dma((3, 4)),
            dma((2,)), dma((4,)),
            dma((4,)), dma((4,)),
            dma((8,)), dma((4,)),
            dma((4,)),
        ],
        compiler_params=pltpu.CompilerParams(
            collective_id=0, has_side_effects=True, vmem_limit_bytes=56 * 1024 * 1024
        ),
        cost_estimate=pl.CostEstimate(flops=14_000_000_000, bytes_accessed=9_000_000, transcendentals=500_000),
        name="window",
    )(
        video.reshape(4, 512, 128),
        frame_counts,
        first_weight.reshape(9, 768, 256),
        second_weight,
        cotangent.reshape(8, 64, 512),
    )
    features, grad_input, grad_first, grad_second = pl.pallas_call(
        finish,
        out_shape=(
            jax.ShapeDtypeStruct((8, 64, 512), bf16),
            jax.ShapeDtypeStruct((4, 512, 128), bf16),
            jax.ShapeDtypeStruct((432, 256), f32),
            jax.ShapeDtypeStruct((96, 512), f32),
        ),
        name="finish",
    )(features, grad_input, first, second)
    return (
        features.reshape(1, 8, 2, 32, 512),
        grad_input.reshape(1, 4, 16, 32, 128),
        grad_first,
        grad_second,
    )


def solution(mesh):
    placed = (
        P("rep", "tm", None, None, None),
        P("rep"),
        P(),
        P(),
        P("rep", None, "tm", None, None),
    )
    return jax.shard_map(
        body,
        mesh=mesh,
        in_specs=placed,
        out_specs=(
            P("rep", None, "tm", None, None),
            P("rep", "tm", None, None, None),
            P("rep", None),
            P("rep", None),
        ),
        check_vma=False,
    )
```
